32 devices in a mesh: row: 8 (over y, x, core), col: 4 (over z).
Axes of the slice: x: 2, y: 2, z: 4, core: 2. Of those that a mesh axis runs over, the one named last changes fastest.
Arguments:
- ancestor: bfloat16 [16384, 16384], P('row', 'col'), as said below
- panels: bfloat16 [3, 8192, 256], P(None, ('row', 'col')), may hold values from -0.625 to 0.625
- row_index: int32 [3, 8192], P(None, ('row', 'col')), may hold values from 0 to 16383, as said below
- diag_inverse: float32 [3, 256, 256], replicated, may hold values from -6 to 6
Outputs:
- off_block: bfloat16 [16384, 768], P(('row', 'col'))
- diag_block: float32 [3, 256, 256], replicated
The draws below stay inside these ranges and needn't reach their ends.
Inputs may be any that keep to these rules, and one draw needn't show every extreme that they name: `row_index`: each of the 3 lists names 8192 different ancestor rows; row 0 and row 16383 are in every list. `ancestor`: entries on and below the diagonal are read; diagonal entries lie between 0.75 and 1.25 plus the off-diagonal spread.
All inputs are finite; a program needn't handle non-finite values.
Results may differ from the reference program's by a relative error of at most 0.014.
Values may be sent and summed in bfloat16 or wider, within the bound.
No kernel may reach another device: no remote copies, remote signals or barrier semaphores. Data moves between devices by JAX's collectives and lax.ppermute only.
A program may use at most 128 MiB of HBM per device.

```python
import jax
import jax.numpy as jnp
from jax import lax

NA = 16384
W = 256
SIBS = 3
RS = 8192
N_ROW = 8
N_COL = 4


def draw_ancestor(key, part):
    key_noise = jax.random.fold_in(key, 0)
    key_diag = jax.random.fold_in(key, 2)
    noise_part = jax.random.normal(key_noise, (NA, NA), jnp.float32)
    matrix = noise_part * (2.0 * RS) ** (-0.5)
    diag_values = 1.0 + 0.25 * jax.random.uniform(key_diag, (NA,), jnp.float32, -1.0, 1.0)
    positions = jnp.arange(NA, dtype=jnp.int32)
    matrix = matrix.at[positions, positions].add(diag_values)
    return matrix.astype(jnp.bfloat16)


def draw_row_index(key, part):
    chosen_lists = []
    for sibling in range(SIBS):
        chosen = jax.random.permutation(jax.random.fold_in(key, 7 + sibling), NA - 2)[:RS - 2] + 1
        complete = jnp.concatenate([jnp.array([0, NA - 1], jnp.int32), chosen.astype(jnp.int32)])
        shuffle_order = jax.random.permutation(jax.random.fold_in(key, 101 + sibling), RS)
        chosen_lists.append(complete[shuffle_order])
    return jnp.stack(chosen_lists).astype(jnp.int32)


def steps_of(rng, shape, cuts, smallest, largest):
    def one(dim, shards_of):
        draws = jax.random.uniform(jax.random.fold_in(jax.random.fold_in(rng, 6), dim), (shards_of,), jnp.float32, smallest / len(cuts), largest / len(cuts))
        return jnp.repeat(jnp.exp(draws), shape[dim] // shards_of).reshape((-1,) + (1,) * (len(shape) - dim - 1))

    loudness = one(*cuts[0])
    for cut in cuts[1:]:
        loudness = loudness * one(*cut)
    return loudness


def gaussian(own_key, dims, width, limit, pieces=(), held_as=jnp.bfloat16):
    result = width * jax.random.normal(own_key, dims, jnp.float32)
    if pieces:
        result = result * steps_of(own_key, dims, pieces, -0.22, 0.18)
    return jnp.clip(result, -limit, limit).astype(held_as)


def setup_inputs(seed: int = 0) -> dict:
    splits = jax.random.split(jax.random.key(seed), 5)
    return {
        "ancestor": draw_ancestor(jax.random.fold_in(splits[4], 71), 0),
        "panels": gaussian(splits[1], (SIBS, RS, W), (4 * RS ** -0.5), 0.625, ((1, 32),)),
        "row_index": draw_row_index(jax.random.fold_in(splits[4], 71), 0),
        "diag_inverse": gaussian(splits[3], (SIBS, W, W), 1.0, 6.0, (), jnp.float32),
    }


def reference(ancestor, panels, row_index, diag_inverse):
    features = SIBS * W
    sibling = jnp.broadcast_to(jnp.arange(SIBS, dtype=jnp.int32)[:, None], row_index.shape)
    spread = jnp.zeros((NA, SIBS, W), jnp.bfloat16).at[row_index, sibling].set(panels)
    member = jnp.zeros((NA, SIBS), jnp.float32).at[row_index, sibling].set(1.0)
    spread_flat = spread.reshape(NA, features)
    block_rows = NA // N_ROW
    block_cols = NA // N_COL
    col_blocks = spread_flat.reshape(N_COL, block_cols, features).astype(jnp.float32)

    def row_block(mirror_sum, block_index):
        first_row = block_index * block_rows
        rows_part = lax.dynamic_slice_in_dim(ancestor, first_row, block_rows, 0)
        row_ids = first_row + lax.broadcasted_iota(jnp.int32, (block_rows, NA), 0)
        col_ids = lax.broadcasted_iota(jnp.int32, (block_rows, NA), 1)
        lower_part = jnp.where(col_ids <= row_ids, rows_part, 0).astype(jnp.float32)
        lower_part = lower_part.reshape(block_rows, N_COL, block_cols)
        strict = jnp.where(col_ids < row_ids, rows_part, 0).astype(jnp.float32)
        strict = strict.reshape(block_rows, N_COL, block_cols)
        direct = jnp.einsum("rcx,cxk->crk", lower_part, col_blocks, precision=lax.Precision.HIGHEST)
        direct = lax.optimization_barrier(direct.astype(jnp.bfloat16)).astype(jnp.float32)
        direct = jnp.sum(direct, axis=0)
        own_spread = lax.dynamic_slice_in_dim(spread_flat, first_row, block_rows, 0).astype(jnp.float32)
        mirrored = jnp.einsum("rcx,rk->cxk", strict, own_spread, precision=lax.Precision.HIGHEST)
        mirrored = lax.optimization_barrier(mirrored.astype(jnp.bfloat16)).astype(jnp.float32)
        return mirror_sum + mirrored.reshape(NA, features), direct

    mirror_sum, direct_rows = lax.scan(row_block, jnp.zeros((NA, features), jnp.float32), jnp.arange(N_ROW, dtype=jnp.int32))
    product = direct_rows.reshape(NA, features) + mirror_sum
    product3 = product.reshape(NA, SIBS, W)
    off_block = jnp.where(member[:, :, None] > 0.5, -product3, 0.0).astype(jnp.bfloat16).reshape(NA, features)
    diag_block = diag_inverse + jnp.einsum("asw,asv->swv", spread.astype(jnp.float32), product3, precision=lax.Precision.HIGHEST)
    return off_block, diag_block
```

```python
import functools

import jax
import jax.numpy as jnp
from jax import lax
from jax.experimental import pallas as pl
from jax.experimental.pallas import tpu as pltpu
from jax.sharding import PartitionSpec as P

LANES = 128
BF = jnp.bfloat16
F32 = jnp.float32


def swap(x, axis, bit):
    count = lax.axis_size(axis)
    return lax.ppermute(x, axis, [(i, i ^ bit) for i in range(count)])


def row_bits(row_count):
    return [b for b in (1 << n for n in range(1, 20)) if b < row_count]


def collect(own, dim):
    col_count = lax.axis_size("col")
    bits = row_bits(lax.axis_size("row"))
    lines = [own] + [swap(own, "col", d) for d in range(1, col_count)]
    first = jnp.concatenate(lines[: col_count // 2], dim)
    second = jnp.concatenate(lines[col_count // 2 :], dim)
    for one, other in zip(bits, bits[::-1]):
        first, second = (
            jnp.concatenate([first, swap(first, "row", one)], dim),
            jnp.concatenate([second, swap(second, "row", other)], dim),
        )
    return [first, second, swap(first, "row", 1), swap(second, "row", 1)], lines


def invert_kernel(index_ref, out_ref):
    sibs, listed = index_ref.shape
    lines = out_ref.shape[1]
    step = min(listed, 2048)
    for s in range(sibs):
        total = jnp.zeros((lines, 2 * LANES), F32)
        for n in range(0, listed, step):
            index = index_ref[s : s + 1, n : n + step]
            place = n + 1 + lax.broadcasted_iota(jnp.int32, (1, step), 1)
            line_of = index // LANES
            lane_of = index % LANES
            high = (place // LANES).astype(F32)
            low = (place % LANES).astype(F32)
            on_line = lax.broadcasted_iota(jnp.int32, (lines, step), 0) == line_of
            on_lane = lax.broadcasted_iota(jnp.int32, (LANES, step), 0) == lane_of
            left = jnp.where(on_line, 1.0, 0.0).astype(BF)
            right = jnp.concatenate(
                [jnp.where(on_lane, high, 0.0), jnp.where(on_lane, low, 0.0)], 0
            ).astype(BF)
            total += lax.dot_general(
                left, right, (((1,), (1,)), ((), ())), preferred_element_type=F32
            )
        out_ref[s] = (total[:, :LANES] * LANES + total[:, LANES:]).astype(jnp.int32)


def invert(index, rows):
    sibs = index.shape[0]
    return pl.pallas_call(
        invert_kernel,
        out_shape=jax.ShapeDtypeStruct((sibs, rows // LANES, LANES), jnp.int32),
        compiler_params=pltpu.CompilerParams(vmem_limit_bytes=32 * 2**20),
        cost_estimate=pl.CostEstimate(
            flops=4 * sibs * rows * index.shape[1], bytes_accessed=4 * sibs * rows, transcendentals=0
        ),
    )(index)


def tables_kernel(
    row_inv, col_inv, p0, p1, p2, p3, row_out, col_out, source, target
):
    step = 256
    width = col_out.shape[1]
    parts = width // LANES
    source[0 : 8 * parts, :] = jnp.zeros((8 * parts, LANES), F32)
    base = 1
    for piece in (p0, p1, p2, p3):
        rows = piece.shape[0]

        def fill(n, unused, piece=piece, base=base):
            at = pl.multiple_of(n * step, step)
            values = piece[pl.ds(at, step), :].astype(F32)
            for q in range(parts):
                source[pl.ds(parts * (base + at) + q, step, stride=parts), :] = values[
                    :, q * LANES : (q + 1) * LANES
                ]
            return unused

        lax.fori_loop(0, rows // step, fill, 0)
        base += rows

    def pick(inv):
        batch = 16

        def line(h, unused):
            for first in range(0, LANES, batch):
                found = [
                    source[pl.ds(pl.multiple_of(parts * inv[h, first + u], parts), parts), :]
                    for u in range(batch)
                ]
                for u in range(batch):
                    target[
                        pl.ds(pl.multiple_of(parts * (h * LANES + first + u), parts), parts), :
                    ] = found[u]
            return unused

        lax.fori_loop(0, inv.shape[0], line, 0)

    pick(row_inv)
    for n in range(row_out.shape[1] // step):
        for q in range(parts):
            values = target[pl.ds(parts * n * step + q, step, stride=parts), :]
            row_out[q * LANES : (q + 1) * LANES, n * step : (n + 1) * step] = values.T.astype(BF)
    pick(col_inv)

    def drain(n, unused):
        at = pl.multiple_of(n * step, step)
        for q in range(parts):
            values = target[pl.ds(parts * at + q, step, stride=parts), :]
            col_out[pl.ds(at, step), q * LANES : (q + 1) * LANES] = values.astype(BF)
        return unused

    lax.fori_loop(0, col_out.shape[0] // step, drain, 0)


def tables(pieces, row_inv, col_inv):
    width = pieces[0].shape[1]
    listed = sum(p.shape[0] for p in pieces)
    parts = width // LANES
    rows, cols = row_inv.size, col_inv.size
    vmem = pl.BlockSpec(memory_space=pltpu.VMEM)
    smem = pl.BlockSpec(memory_space=pltpu.SMEM)
    return pl.pallas_call(
        tables_kernel,
        in_specs=[smem, smem] + [vmem] * 4,
        out_specs=[vmem, vmem],
        out_shape=[
            jax.ShapeDtypeStruct((width, rows), BF),
            jax.ShapeDtypeStruct((cols, width), BF),
        ],
        scratch_shapes=[
            pltpu.VMEM((parts * (listed + 8), LANES), F32),
            pltpu.VMEM((parts * max(rows, cols), LANES), F32),
        ],
        compiler_params=pltpu.CompilerParams(vmem_limit_bytes=48 * 2**20),
        cost_estimate=pl.CostEstimate(
            flops=10**10, bytes_accessed=2 * width * (listed + rows + cols), transcendentals=0
        ),
    )(row_inv, col_inv, *pieces)


def terms_kernel(
    plan, block, row_t, col, m_send, m_keep, d_send, d_keep, y_send, y_keep, total, mirror_y, lower, strict
):
    i = pl.program_id(0)
    steps = pl.num_programs(0)
    tile = block.shape[1]
    rows = block.shape[0]
    row_start = plan[steps]
    first_col = plan[steps + 1] + plan[i] * tile

    @pl.when(i == 0)
    def start():
        total[...] = jnp.zeros_like(total)
        mirror_y[...] = jnp.zeros_like(mirror_y)

    def work(low_ref, strict_ref):
        mirrored = jnp.dot(row_t[...], strict_ref[...], preferred_element_type=F32).astype(BF)

        @pl.when(i < steps // 2)
        def sent():
            m_send[0] = mirrored

        @pl.when(i >= steps // 2)
        def kept():
            m_keep[0] = mirrored

        mirror_y[...] += jnp.dot(mirrored, col[...], preferred_element_type=F32)
        step = 256

        def direct(n, unused):
            at = pl.ds(pl.multiple_of(n * step, step), step)
            total[at, :] += jnp.dot(low_ref[at, :], col[...], preferred_element_type=F32)
            return unused

        lax.fori_loop(0, rows // step, direct, 0)

    full = row_start >= first_col + tile
    none = row_start + rows <= first_col

    @pl.when(full)
    def whole():
        work(block, block)

    @pl.when(jnp.logical_not(jnp.logical_or(full, none)))
    def cut():
        step = 256

        def mask(n, unused):
            at = pl.ds(pl.multiple_of(n * step, step), step)
            row_ids = row_start + n * step + lax.broadcasted_iota(jnp.int32, (step, tile), 0)
            col_ids = first_col + lax.broadcasted_iota(jnp.int32, (step, tile), 1)
            values = block[at, :]
            nothing = jnp.zeros((), BF)
            lower[at, :] = jnp.where(col_ids <= row_ids, values, nothing)
            strict[at, :] = jnp.where(col_ids < row_ids, values, nothing)
            return unused

        lax.fori_loop(0, rows // step, mask, 0)
        work(lower, strict)

    @pl.when(none)
    def nothing_here():
        zero = jnp.zeros(m_send.shape[1:], BF)

        @pl.when(i < steps // 2)
        def sent():
            m_send[0] = zero

        @pl.when(i >= steps // 2)
        def kept():
            m_keep[0] = zero

    @pl.when(i == steps - 1)
    def finish():
        owned = d_send.shape[1]
        count = rows // owned
        place = plan[steps + 2]
        direct_y = jnp.zeros(mirror_y.shape, F32)
        for e in range(count):
            at = pl.multiple_of((e ^ place) * owned, owned)
            term = total[pl.ds(at, owned), :].astype(BF)
            if e % 2:
                d_send[e // 2] = term
            else:
                d_keep[e // 2] = term
            direct_y += jnp.dot(row_t[:, pl.ds(at, owned)], term, preferred_element_type=F32)
        y = direct_y + mirror_y[...].T
        half = y.shape[0] // 2
        core = plan[steps + 3]

        @pl.when(core == 0)
        def first_core():
            y_keep[...] = y[:half]
            y_send[...] = y[half:]

        @pl.when(core != 0)
        def second_core():
            y_keep[...] = y[half:]
            y_send[...] = y[:half]


def terms(plan, ancestor, row_t, col, owned):
    rows, cols = ancestor.shape
    width = col.shape[1]
    steps = cols // owned
    count = rows // owned
    half = steps // 2
    grid_spec = pltpu.PrefetchScalarGridSpec(
        num_scalar_prefetch=1,
        grid=(steps,),
        in_specs=[
            pl.BlockSpec((rows, owned), lambda i, plan: (0, plan[i])),
            pl.BlockSpec((width, rows), lambda i, plan: (0, 0)),
            pl.BlockSpec((owned, width), lambda i, plan: (plan[i], 0)),
        ],
        out_specs=[
            pl.BlockSpec((1, width, owned), lambda i, plan: (jnp.minimum(i, half - 1), 0, 0)),
            pl.BlockSpec((1, width, owned), lambda i, plan: (jnp.maximum(i - half, 0), 0, 0)),
            pl.BlockSpec((count // 2, owned, width), lambda i, plan: (0, 0, 0)),
            pl.BlockSpec((count // 2, owned, width), lambda i, plan: (0, 0, 0)),
            pl.BlockSpec((width // 2, width), lambda i, plan: (0, 0)),
            pl.BlockSpec((width // 2, width), lambda i, plan: (0, 0)),
        ],
        scratch_shapes=[
            pltpu.VMEM((rows, width), F32),
            pltpu.VMEM((width, width), F32),
            pltpu.VMEM((rows, owned), BF),
            pltpu.VMEM((rows, owned), BF),
        ],
    )
    return pl.pallas_call(
        terms_kernel,
        grid_spec=grid_spec,
        out_shape=[
            jax.ShapeDtypeStruct((half, width, owned), BF),
            jax.ShapeDtypeStruct((half, width, owned), BF),
            jax.ShapeDtypeStruct((count // 2, owned, width), BF),
            jax.ShapeDtypeStruct((count // 2, owned, width), BF),
            jax.ShapeDtypeStruct((width // 2, width), F32),
            jax.ShapeDtypeStruct((width // 2, width), F32),
        ],
        compiler_params=pltpu.CompilerParams(vmem_limit_bytes=56 * 2**20),
        cost_estimate=pl.CostEstimate(
            flops=4 * rows * cols * width, bytes_accessed=2 * rows * cols, transcendentals=0
        ),
    )(plan, ancestor, row_t, col)


def add(a, b):
    return (a.astype(F32) + b.astype(F32)).astype(a.dtype)


def halve(values, bits, axis, labels, shift):
    for bit in bits:
        at = labels.index(bit)
        sent = lax.index_in_dim(values, 1, at, keepdims=False)
        kept = lax.index_in_dim(values, 0, at, keepdims=False)
        labels = labels[:at] + labels[at + 1 :]
        values = add(kept, swap(sent, axis, bit << shift))
    return values


def reversed_bits(value, bits):
    return sum(((value >> n) & 1) << (bits - 1 - n) for n in range(bits))


def to_owner(x):
    row_count = lax.axis_size("row")
    col_count = lax.axis_size("col")
    bits = col_count.bit_length() - 1
    pairs = []
    for row in range(row_count):
        for col in range(col_count):
            place = (row // 2) ^ reversed_bits(col, bits)
            pairs.append((row * col_count + col, (2 * col + row % 2) * col_count + place))
    return lax.ppermute(x, ("row", "col"), pairs)


def per_device(ancestor, panels, row_index, diag_inverse):
    row_count = lax.axis_size("row")
    col_count = lax.axis_size("col")
    assert row_count == 2 * col_count
    block_rows, block_cols = ancestor.shape
    sib_count, _, width = panels.shape
    owned = block_rows // col_count
    row_place = lax.axis_index("row")
    col_place = lax.axis_index("col")
    core = row_place % 2
    chip = row_place // 2
    col_bits = col_count.bit_length() - 1

    index_pieces, _ = collect(row_index, 1)
    inverse = invert(jnp.concatenate(index_pieces, 1), block_rows * row_count)
    row_inv = lax.dynamic_slice_in_dim(
        inverse, row_place * (block_rows // LANES), block_rows // LANES, 1
    )
    col_inv = lax.dynamic_slice_in_dim(
        inverse, col_place * (block_cols // LANES), block_cols // LANES, 1
    )
    own_inv = lax.dynamic_slice_in_dim(
        inverse, row_place * (block_rows // LANES) + col_place * (owned // LANES), owned // LANES, 1
    )
    member = own_inv.reshape(sib_count, owned) > 0

    slots = jnp.arange(col_count, dtype=jnp.int32)
    mixed = sum(((col_place >> n) & 1) << (col_bits - 1 - n) for n in range(col_bits))
    places = slots ^ (chip ^ mixed).astype(jnp.int32)
    plan = jnp.concatenate(
        [
            places + (1 - core) * col_count,
            places + core * col_count,
            jnp.stack([row_place * block_rows, col_place * block_cols, col_place, core]),
        ]
    ).astype(jnp.int32)

    before = None
    offs = []
    diags = []
    for s in range(sib_count):
        own = panels[s]
        if before is not None:
            own, _ = lax.optimization_barrier((own, before))
        pieces, before = collect(own, 0)
        row_t, col = tables(pieces, row_inv[s], col_inv[s])
        m_send, m_keep, d_send, d_keep, y_send, y_keep = terms(plan, ancestor, row_t, col, owned)

        m_got = swap(m_send, "row", 1)
        d_got = swap(d_send, "col", 1)
        mirrored = add(m_keep, m_got).reshape((2,) * col_bits + (2, width // 2, owned))
        labels = [1 << n for n in range(col_bits)][::-1]
        first = lax.index_in_dim(mirrored, 0, col_bits, keepdims=False)
        second = lax.index_in_dim(mirrored, 1, col_bits, keepdims=False)
        first = halve(first, labels[::-1], "row", labels, 1)
        second = halve(second, labels, "row", labels, 1)
        first, second = to_owner(first), to_owner(second)

        direct = add(d_keep, d_got).reshape((2,) * (col_bits - 1) + (owned, width))
        labels = [1 << n for n in range(1, col_bits)][::-1]
        for bit in labels[:0:-1]:
            at = labels.index(bit)
            sent = lax.index_in_dim(direct, 1, at, keepdims=False)
            kept = lax.index_in_dim(direct, 0, at, keepdims=False)
            labels = labels[:at] + labels[at + 1 :]
            direct = add(kept, swap(sent, "col", bit))
        got = swap(direct[1], "col", labels[0])
        product = (
            direct[0].astype(F32)
            + got.astype(F32)
            + jnp.concatenate([first, second], 0).astype(F32).T
        )
        offs.append(jnp.where(member[s][:, None], -product, 0.0).astype(BF))

        y = y_keep + swap(y_send, "row", 1)
        for bit in row_bits(row_count):
            y = y + swap(y, "row", bit)
        for n in range(col_bits):
            y = y + swap(y, "col", 1 << n)
        other = swap(y, "row", 1)
        diags.append(
            jnp.where(core == 0, jnp.concatenate([y, other], 0), jnp.concatenate([other, y], 0))
        )
    return jnp.concatenate(offs, 1), diag_inverse + jnp.stack(diags)


def solution(mesh):
    in_specs = (P("row", "col"), P(None, ("row", "col"), None), P(None, ("row", "col")), P())
    out_specs = (P(("row", "col"), None), P())
    return jax.shard_map(
        per_device, mesh=mesh, in_specs=in_specs, out_specs=out_specs, check_vma=False
    )
```

```python
import functools

import jax
import jax.numpy as jnp
from jax import lax
from jax.experimental import pallas as pl
from jax.experimental.pallas import tpu as pltpu
from jax.sharding import PartitionSpec as P

LANES = 128
BF = jnp.bfloat16
F32 = jnp.float32


def swap(x, axis, bit):
    count = lax.axis_size(axis)
    return lax.ppermute(x, axis, [(i, i ^ bit) for i in range(count)])


def row_bits(row_count):
    return [b for b in (1 << n for n in range(1, 20)) if b < row_count]


def join_kernel(counts, *refs):
    outs = refs[len(refs) - len(counts) :]
    refs = iter(refs)
    for count, out in zip(counts, outs):
        at = 0
        for _ in range(count):
            ref = next(refs)
            out[at : at + ref.shape[0]] = ref[...]
            at += ref.shape[0]


def join(groups, marks=()):
    flat = [x for group in groups for x in group]
    vmem = pl.BlockSpec(memory_space=pltpu.VMEM)
    size = 2 * sum(x.size for x in flat)
    return pl.pallas_call(
        functools.partial(join_kernel, [len(group) for group in groups]),
        in_specs=[vmem] * (len(flat) + len(marks)),
        out_specs=[vmem] * len(groups),
        out_shape=[
            jax.ShapeDtypeStruct((sum(x.shape[0] for x in group), group[0].shape[1]), BF)
            for group in groups
        ],
        compiler_params=pltpu.CompilerParams(vmem_limit_bytes=24 * 2**20),
        cost_estimate=pl.CostEstimate(flops=0, bytes_accessed=2 * size, transcendentals=0),
    )(*flat, *marks)


def gather(owns, marks):
    col_count = lax.axis_size("col")
    bits = row_bits(lax.axis_size("row"))
    half = col_count // 2
    rounds = len(bits) + 1
    state = [None] * len(owns)
    sent = owns[0]
    for tick in range(rounds + len(owns) - 1):
        groups, places = [], []
        for n in range(len(owns)):
            step = tick - n
            if step == 0:
                line = [sent] + [swap(sent, "col", d) for d in range(1, col_count)]
                state[n] = [line[:half], line[half:]]
            elif 0 < step < rounds:
                first, second = state[n]
                state[n] = [
                    [first, swap(first, "row", bits[step - 1])],
                    [second, swap(second, "row", bits[-step])],
                ]
            else:
                continue
            for side in range(2):
                places.append((n, side))
                groups.append(state[n][side])
        if tick + 1 < len(owns):
            groups.append([owns[tick + 1]])
        joined = join(groups, tuple(marks[tick : tick + 1]))
        if tick + 1 < len(owns):
            sent = joined[-1]
        for (n, side), value in zip(places, joined):
            state[n][side] = value
        done = tick - rounds + 1
        if done >= 0:
            first, second = state[done]
            yield [first, second, swap(first, "row", 1), swap(second, "row", 1)]


def invert_kernel(listed, sibs, p0, p1, p2, p3, out_ref):
    pieces = (p0, p1, p2, p3)
    lines = out_ref.shape[1]
    count, _, wide = p0.shape
    line_ids = lax.broadcasted_iota(jnp.int32, (lines, wide), 0).astype(F32)
    lane_ids = lax.broadcasted_iota(jnp.int32, (LANES, wide), 0).astype(F32)
    for s in range(sibs):
        total = jnp.zeros((lines, 2 * LANES), F32)
        for n, piece in enumerate(pieces):
            left, right = [], []
            for m in range(count):
                code = piece[m, listed:, :].astype(F32)
                place = 1 + (n * count + m) * listed
                place = place + lax.broadcasted_iota(jnp.int32, (1, wide), 1)
                high = (place // LANES).astype(F32)
                low = (place % LANES).astype(F32)
                left.append(jnp.where(line_ids == code[2 * s : 2 * s + 1], 1.0, 0.0))
                on_lane = lane_ids == code[2 * s + 1 : 2 * s + 2]
                right.append(
                    jnp.concatenate(
                        [jnp.where(on_lane, high, 0.0), jnp.where(on_lane, low, 0.0)], 0
                    )
                )
            total += lax.dot_general(
                jnp.concatenate(left, 1).astype(BF),
                jnp.concatenate(right, 1).astype(BF),
                (((1,), (1,)), ((), ())),
                preferred_element_type=F32,
            )
        out_ref[s] = (total[:, :LANES] * LANES + total[:, LANES:]).astype(jnp.int32)


def invert(pieces, chunk, codes, sibs, rows):
    width = pieces[0].shape[1]
    pieces = [p.reshape(-1, chunk + codes, width) for p in pieces]
    vmem = pl.BlockSpec(memory_space=pltpu.VMEM)
    return pl.pallas_call(
        functools.partial(invert_kernel, chunk, sibs),
        in_specs=[vmem] * 4,
        out_specs=pl.BlockSpec(memory_space=pltpu.VMEM),
        out_shape=jax.ShapeDtypeStruct((sibs, rows // LANES, LANES), jnp.int32),
        compiler_params=pltpu.CompilerParams(vmem_limit_bytes=16 * 2**20),
        cost_estimate=pl.CostEstimate(
            flops=4 * 10**9, bytes_accessed=4 * sibs * rows, transcendentals=0
        ),
    )(*pieces)


def tables_kernel(chunk, row_inv, col_inv, p0, p1, p2, p3, *refs):
    row_out, col_out, mark, source, target = refs[-5:]
    mark[...] = jnp.zeros_like(mark)
    step = 256
    width = col_out.shape[1]
    parts = width // LANES
    count = p0.shape[0]
    source[0 : 8 * parts, :] = jnp.zeros((8 * parts, LANES), F32)
    for n, piece in enumerate((p0, p1, p2, p3)):

        def fill(m, unused, n=n, piece=piece):
            values = piece[m, :chunk, :].astype(F32)
            base = parts * (1 + (n * count + m) * chunk)
            for q in range(parts):
                source[pl.ds(base + q, chunk, stride=parts), :] = values[
                    :, q * LANES : (q + 1) * LANES
                ]
            return unused

        lax.fori_loop(0, count, fill, 0)

    def pick(inv):
        batch = 16

        def line(h, unused):
            for first in range(0, LANES, batch):
                found = [
                    source[pl.ds(pl.multiple_of(parts * inv[h, first + u], parts), parts), :]
                    for u in range(batch)
                ]
                for u in range(batch):
                    target[
                        pl.ds(pl.multiple_of(parts * (h * LANES + first + u), parts), parts), :
                    ] = found[u]
            return unused

        lax.fori_loop(0, inv.shape[0], line, 0)

    pick(row_inv)
    for n in range(row_out.shape[1] // step):
        for q in range(parts):
            values = target[pl.ds(parts * n * step + q, step, stride=parts), :]
            row_out[q * LANES : (q + 1) * LANES, n * step : (n + 1) * step] = values.T.astype(BF)
    pick(col_inv)

    def drain(n, unused):
        at = pl.multiple_of(n * step, step)
        for q in range(parts):
            values = target[pl.ds(parts * at + q, step, stride=parts), :]
            col_out[pl.ds(at, step), q * LANES : (q + 1) * LANES] = values.astype(BF)
        return unused

    lax.fori_loop(0, col_out.shape[0] // step, drain, 0)


def tables(pieces, chunk, whole_chunk, row_inv, col_inv, marks):
    width = pieces[0].shape[1]
    pieces = [p.reshape(-1, whole_chunk, width) for p in pieces]
    count = pieces[0].shape[0]
    listed = 4 * count * chunk
    parts = width // LANES
    rows, cols = row_inv.size, col_inv.size
    vmem = pl.BlockSpec(memory_space=pltpu.VMEM)
    smem = pl.BlockSpec(memory_space=pltpu.SMEM)
    return pl.pallas_call(
        functools.partial(tables_kernel, chunk),
        in_specs=[smem, smem] + [vmem] * (4 + len(marks)),
        out_specs=[vmem] * 3,
        out_shape=[
            jax.ShapeDtypeStruct((width, rows), BF),
            jax.ShapeDtypeStruct((cols, width), BF),
            jax.ShapeDtypeStruct((8, LANES), F32),
        ],
        scratch_shapes=[
            pltpu.VMEM((parts * (listed + 8), LANES), F32),
            pltpu.VMEM((parts * max(rows, cols), LANES), F32),
        ],
        compiler_params=pltpu.CompilerParams(vmem_limit_bytes=28 * 2**20),
        cost_estimate=pl.CostEstimate(
            flops=10**10, bytes_accessed=2 * width * (listed + rows + cols), transcendentals=0
        ),
    )(row_inv, col_inv, *pieces, *marks)


def block_kernel(ancestor, lower, diagonal, mark, held, arrived, left):
    mark[...] = jnp.zeros_like(mark)
    rows, cols = lower.shape
    step = 256
    wide = 512 if cols % 512 == 0 else cols
    row_start = lax.axis_index("row") * rows
    col_start = lax.axis_index("col") * cols
    ins, outs = [], []
    for n in range(0, rows, step):
        here = held.at[n : n + step]
        ins.append(pltpu.make_async_copy(ancestor.at[n : n + step], here, arrived.at[n // step]))
        outs.append(pltpu.make_async_copy(here, lower.at[n : n + step], left.at[n // step]))
    for copy in ins:
        copy.start()
    diagonal[...] = jnp.zeros_like(diagonal)
    for n in range(rows // step):
        ins[n].wait()
        row_first = row_start + n * step
        at = slice(n * step, (n + 1) * step)

        def strip(m, unused, row_first=row_first, at=at):
            first = pl.multiple_of(m * wide, wide)
            over = pl.ds(first, wide)
            col_first = col_start + first
            empty = row_first + step <= col_first

            @pl.when(empty)
            def none():
                held[at, over] = jnp.zeros((step, wide), BF)

            @pl.when(jnp.logical_not(empty) & (row_first < col_first + wide))
            def some():
                row_ids = row_first + lax.broadcasted_iota(jnp.int32, (step, wide), 0)
                col_ids = col_first + lax.broadcasted_iota(jnp.int32, (step, wide), 1)
                values = held[at, over].astype(F32)
                on = jnp.where(col_ids == row_ids, values, 0.0)
                diagonal[at, :] += jnp.sum(on, axis=1, keepdims=True)
                held[at, over] = jnp.where(col_ids < row_ids, values, 0.0).astype(BF)

            return unused

        lax.fori_loop(0, cols // wide, strip, 0)
        outs[n].start()
    for copy in outs:
        copy.wait()


def lower_block(ancestor):
    rows, cols = ancestor.shape
    anywhere = pl.BlockSpec(memory_space=pl.ANY)
    return pl.pallas_call(
        block_kernel,
        in_specs=[anywhere],
        out_specs=[pl.BlockSpec(memory_space=pltpu.HBM)] + [pl.BlockSpec(memory_space=pltpu.VMEM)] * 2,
        out_shape=[
            jax.ShapeDtypeStruct((rows, cols), BF),
            jax.ShapeDtypeStruct((rows, 1), F32),
            jax.ShapeDtypeStruct((8, LANES), F32),
        ],
        scratch_shapes=[
            pltpu.VMEM((rows, cols), BF),
            pltpu.SemaphoreType.DMA((rows // 256,)),
            pltpu.SemaphoreType.DMA((rows // 256,)),
        ],
        compiler_params=pltpu.CompilerParams(vmem_limit_bytes=24 * 2**20),
        cost_estimate=pl.CostEstimate(
            flops=rows * cols, bytes_accessed=4 * rows * cols, transcendentals=0
        ),
    )(ancestor)


def terms_kernel(plan, block, diagonal, row_t, col, *refs):
    m_send, m_keep, d_send, d_keep, y_send, y_keep, total, rounded = refs[-8:]
    i = pl.program_id(0)
    steps = pl.num_programs(0)
    rows = block.shape[0]
    owned = m_send.shape[2]
    tile = 2 * owned
    width = row_t.shape[0]
    place, core, swapped, offset = [plan[steps + n] for n in range(4)]
    at_tile = pl.ds(pl.multiple_of(plan[i] * tile, tile), tile)
    values = col[at_tile, :]

    def mirrored(out):
        term = jnp.dot(row_t[...], block[...], preferred_element_type=F32).astype(BF)
        out[swapped] = term[:, :owned]
        out[1 - swapped] = term[:, owned:]

    @pl.when(i < steps // 2)
    def sent():
        mirrored(m_send)

    @pl.when(i >= steps // 2)
    def kept():
        mirrored(m_keep)

    @pl.when(i == 0)
    def first():
        total[...] = jnp.dot(block[...], values, preferred_element_type=F32)

    @pl.when(i > 0)
    def later():
        total[...] += jnp.dot(block[...], values, preferred_element_type=F32)

    @pl.when(i == steps - 1)
    def last():
        cols = col.shape[0]
        for e in range(rows // owned):
            start = pl.multiple_of((e ^ place) * owned, owned)
            at = pl.ds(start, owned)
            back = pl.multiple_of(jnp.clip(start + offset, 0, cols - owned), owned)
            own = diagonal[at, :] * col[pl.ds(back, owned), :].astype(F32)
            term = total[at, :]
            rounded[at, :] = (term + 0.5 * own).astype(BF)
            term = (term + own).astype(BF)
            if e % 2:
                d_send[e // 2] = term
            else:
                d_keep[e // 2] = term
        y = jnp.dot(row_t[...], rounded[...], preferred_element_type=F32)
        y = y + y.T
        half = width // 2

        @pl.when(core == 0)
        def first_core():
            y_keep[0] = y[:half]
            y_send[0] = y[half:]

        @pl.when(core != 0)
        def second_core():
            y_keep[0] = y[half:]
            y_send[0] = y[:half]


def terms(plan, lower, diagonal, row_t, col, owned, marks):
    rows, cols = lower.shape
    width = col.shape[1]
    steps = cols // (2 * owned)
    half = steps // 2
    count = rows // owned
    everything = [
        pl.BlockSpec(x.shape, lambda i, plan, x=x: (0,) * x.ndim) for x in (diagonal, row_t, col)
    ]
    anywhere = pl.BlockSpec(memory_space=pl.ANY)
    d_spec = pl.BlockSpec((count // 2, owned, width), lambda i, plan: (0, 0, 0))
    y_spec = pl.BlockSpec((1, width // 2, width), lambda i, plan: (0, 0, 0))
    grid_spec = pltpu.PrefetchScalarGridSpec(
        num_scalar_prefetch=1,
        grid=(steps,),
        in_specs=[pl.BlockSpec((rows, 2 * owned), lambda i, plan: (0, plan[i]))]
        + everything
        + [anywhere] * len(marks),
        out_specs=[
            pl.BlockSpec((2, width, owned), lambda i, plan: (jnp.minimum(i, half - 1), 0, 0)),
            pl.BlockSpec((2, width, owned), lambda i, plan: (jnp.maximum(i - half, 0), 0, 0)),
            d_spec,
            d_spec,
            y_spec,
            y_spec,
        ],
        scratch_shapes=[pltpu.VMEM((rows, width), F32), pltpu.VMEM((rows, width), BF)],
    )
    return pl.pallas_call(
        terms_kernel,
        grid_spec=grid_spec,
        out_shape=[
            jax.ShapeDtypeStruct((steps, width, owned), BF),
            jax.ShapeDtypeStruct((steps, width, owned), BF),
            jax.ShapeDtypeStruct((count // 2, owned, width), BF),
            jax.ShapeDtypeStruct((count // 2, owned, width), BF),
            jax.ShapeDtypeStruct((1, width // 2, width), F32),
            jax.ShapeDtypeStruct((1, width // 2, width), F32),
        ],
        compiler_params=pltpu.CompilerParams(vmem_limit_bytes=34 * 2**20),
        cost_estimate=pl.CostEstimate(
            flops=5 * rows * cols * width, bytes_accessed=2 * rows * cols, transcendentals=0
        ),
    )(plan, lower, diagonal, row_t, col, *marks)


def tree_sum(values):
    values = [x.astype(F32) for x in values]
    while len(values) > 1:
        values = [a + b for a, b in zip(values[::2], values[1::2])]
    return values[0]


def sums_kernel(counts, outs, *refs):
    ins, outs_refs = refs[: len(refs) - len(outs)], refs[len(refs) - len(outs) :]
    groups, at = [], 0
    for count in counts:
        groups.append(ins[at : at + count])
        at += count
    for ref, pieces in zip(outs_refs, outs):
        for place, group, slot, low, high in pieces:
            ref[place] = tree_sum([x[slot, low:high] for x in groups[group]]).astype(ref.dtype)


def sums(groups, outs):
    flat = [x for group in groups for x in group]
    shapes = []
    for pieces in outs:
        _, group, _, low, high = pieces[0]
        like = groups[group][0]
        shapes.append(
            jax.ShapeDtypeStruct((len(pieces), high - low, like.shape[2]), like.dtype)
        )
    vmem = pl.BlockSpec(memory_space=pltpu.VMEM)
    size = sum(x.size for x in flat)
    return pl.pallas_call(
        functools.partial(sums_kernel, [len(group) for group in groups], outs),
        in_specs=[vmem] * len(flat),
        out_specs=[vmem] * len(outs),
        out_shape=shapes,
        compiler_params=pltpu.CompilerParams(vmem_limit_bytes=16 * 2**20),
        cost_estimate=pl.CostEstimate(flops=size, bytes_accessed=3 * size, transcendentals=0),
    )(*flat)


def mirrored_share(m_send, m_keep, paths):
    col_bits = lax.axis_size("col").bit_length() - 1
    width, owned = m_keep.shape[1:]
    part = width // paths
    bits = row_bits(lax.axis_size("row"))
    slots = [list(range(len(m_keep))) for _ in range(paths)]
    groups = [(m_keep, swap(m_send, "row", 1))]
    for n in range(col_bits):
        outs = []
        chosen_bits = []
        for path in range(paths):
            place = col_bits - 1 - n if path else n
            chosen_bits.append(bits[place])
            low, group = (part * path, 0) if n == 0 else (0, path)
            for send in (True, False):
                chosen = [i for i, e in enumerate(slots[path]) if bool(e >> place & 1) == send]
                outs.append([(p, group, i, low, low + part) for p, i in enumerate(chosen)])
            slots[path] = [e for e in slots[path] if not e >> place & 1]
        made = yield groups, outs
        groups = [
            (made[2 * path + 1], swap(made[2 * path], "row", chosen_bits[path]))
            for path in range(paths)
        ]
    (own,) = yield groups, [[(path, path, 0, 0, part) for path in range(paths)]]
    return to_owner(own.reshape(width, owned))


def direct_share(d_send, d_keep):
    col_bits = lax.axis_size("col").bit_length() - 1
    owned = d_keep.shape[1]
    groups = [(d_keep, swap(d_send, "col", 1))]
    slots = list(range(len(d_keep)))
    for n in range(1, col_bits):
        bit = 1 << (n - 1)
        outs = []
        for send in (True, False):
            chosen = [i for i, e in enumerate(slots) if bool(e & bit) == send]
            outs.append([(p, 0, i, 0, owned) for p, i in enumerate(chosen)])
        slots = [e for e in slots if not e & bit]
        d_send, d_keep = yield groups, outs
        groups = [(d_keep, swap(d_send, "col", bit << 1))]
    return groups[0]


def diagonal_sum(y_send, y_keep, core, direct):
    rows = y_keep.shape[1]
    whole = [[(0, 0, 0, 0, rows)]]
    (y,) = yield [(y_keep, swap(y_send, "row", 1))], whole
    for axis, first in (("row", 2), ("col", 1)):
        size = lax.axis_size(axis)
        if direct:
            steps = [range(first, size, first)]
        else:
            steps = [[first << n] for n in range((size // first).bit_length() - 1)]
        for step in steps:
            (y,) = yield [(y, *[swap(y, axis, bits) for bits in step])], whole
    other = swap(y, "row", 1)[0]
    return jnp.where(
        core == 0, jnp.concatenate([y[0], other], 0), jnp.concatenate([other, y[0]], 0)
    )


class Rounds:
    def __init__(self, *chains):
        self.chains = chains
        self.results = [None] * len(chains)
        self.jobs = {}
        for n, chain in enumerate(chains):
            self.send(n, None)

    def send(self, n, values):
        try:
            self.jobs[n] = self.chains[n].send(values)
        except StopIteration as end:
            self.jobs.pop(n, None)
            self.results[n] = end.value

    def advance(self):
        groups, outs = [], []
        for job_groups, job_outs in self.jobs.values():
            for pieces in job_outs:
                outs.append([(p, group + len(groups), *rest) for p, group, *rest in pieces])
            groups += job_groups
        made = sums(groups, outs)
        at = 0
        for n, (_, job_outs) in list(self.jobs.items()):
            self.send(n, made[at : at + len(job_outs)])
            at += len(job_outs)
        return made[-1]

    def finish(self):
        while self.jobs:
            self.advance()
        return self.results


def reversed_bits(value, bits):
    return sum(((value >> n) & 1) << (bits - 1 - n) for n in range(bits))


def to_owner(x):
    row_count = lax.axis_size("row")
    col_count = lax.axis_size("col")
    bits = col_count.bit_length() - 1
    pairs = []
    for row in range(row_count):
        for col in range(col_count):
            place = (row // 2) ^ reversed_bits(col, bits)
            pairs.append((row * col_count + col, (2 * col + row % 2) * col_count + place))
    return lax.ppermute(x, ("row", "col"), pairs)


def finish_kernel(member, *refs):
    out = refs[-1]
    owned = out.shape[0]
    sibs = member.shape[0]
    width = out.shape[1] // sibs
    s = 0
    for n in range(0, len(refs) - 1, 3):
        kept, got, mirrored = refs[n : n + 3]
        for at in range(0, mirrored.shape[0], width):
            over = slice(at, at + width)
            product = kept[0, :, over].astype(F32) + got[0, :, over].astype(F32)
            product = product + mirrored[over, :].astype(F32).T
            listed = jnp.broadcast_to(member[s : s + 1, :].astype(F32), (LANES, owned)).T
            for q in range(0, width, LANES):
                out[:, s * width + q : s * width + q + LANES] = jnp.where(
                    listed > 0.5, -product[:, q : q + LANES], 0.0
                ).astype(BF)
            s += 1


def finish(member, shares, width):
    sibs, owned = member.shape
    vmem = pl.BlockSpec(memory_space=pltpu.VMEM)
    flat = [x for share in shares for x in share]
    return pl.pallas_call(
        finish_kernel,
        in_specs=[vmem] * (1 + len(flat)),
        out_specs=vmem,
        out_shape=jax.ShapeDtypeStruct((owned, sibs * width), BF),
        compiler_params=pltpu.CompilerParams(vmem_limit_bytes=24 * 2**20),
        cost_estimate=pl.CostEstimate(
            flops=4 * owned * sibs * width,
            bytes_accessed=8 * owned * sibs * width,
            transcendentals=0,
        ),
    )(member, *flat)


def per_device(ancestor, panels, row_index, diag_inverse):
    row_count = lax.axis_size("row")
    col_count = lax.axis_size("col")
    assert row_count == 2 * col_count
    block_rows, block_cols = ancestor.shape
    sib_count, listed, width = panels.shape
    owned = block_rows // col_count
    row_place = lax.axis_index("row")
    col_place = lax.axis_index("col")
    core = row_place % 2
    chip = row_place // 2
    col_bits = col_count.bit_length() - 1
    row_lines, col_lines, own_lines = block_rows // LANES, block_cols // LANES, owned // LANES
    mixed = chip ^ sum(((col_place >> n) & 1) << (col_bits - 1 - n) for n in range(col_bits))
    pairs = [(2 * n ^ mixed) // 2 for n in range(col_count // 2)]
    plan = jnp.stack(
        [n + (1 - core) * (col_count // 2) for n in pairs]
        + [n + core * (col_count // 2) for n in pairs]
        + [col_place, core, mixed % 2, row_place * block_rows - col_place * block_cols]
    ).astype(jnp.int32)

    codes = jnp.stack([row_index // LANES, row_index % LANES], 1).astype(BF)
    codes = codes.reshape(-1, listed)
    code_rows = -(-len(codes) // 16) * 16
    codes = jnp.pad(
        codes, ((0, code_rows - len(codes)), (0, width - listed)), constant_values=-1
    )
    owns = [jnp.concatenate([panels[0], codes], 0)] + [panels[s] for s in range(1, sib_count)]
    chunks = [listed + code_rows] + [listed] * (sib_count - 1)

    lower, diagonal, mark = lower_block(ancestor)
    marks = [mark] * (len(row_bits(row_count)) + 1)
    gathered = gather(owns, marks)
    both, direct = [], []
    tables_marks, terms_marks = [()] * 2, [()] * 2
    row_inv = col_inv = member = None
    for s in range(sib_count):
        pieces = next(gathered)
        if s == 0:
            inverse = invert(pieces, listed, code_rows, sib_count, block_rows * row_count)
            row_inv = lax.dynamic_slice_in_dim(inverse, row_place * row_lines, row_lines, 1)
            col_inv = lax.dynamic_slice_in_dim(inverse, col_place * col_lines, col_lines, 1)
            own_inv = lax.dynamic_slice_in_dim(
                inverse, row_place * row_lines + col_place * own_lines, own_lines, 1
            )
            member = own_inv.reshape(sib_count, owned)
        last = s == sib_count - 1
        before = ()
        if s > 1:
            before = tuple(chain.advance() for chain in both[:-1] + direct[:-1] if chain.jobs)
        row_t, col, mark = tables(pieces, listed, chunks[s], row_inv[s], col_inv[s], before)
        before = tuple(chain.advance() for chain in both if chain.jobs)
        m_send, m_keep, d_send, d_keep, y_send, y_keep = terms(
            plan, lower, diagonal, row_t, col, owned, before
        )
        marks.append(mark)
        both.append(
            Rounds(
                mirrored_share(m_send, m_keep, 2 if last else 1),
                diagonal_sum(y_send, y_keep, core, last),
            )
        )
        direct.append(Rounds(direct_share(d_send, d_keep)))
    shares, diags = [], []
    for s in range(sib_count):
        mirrored, diag = both[s].finish()
        shares.append((*direct[s].finish()[0], mirrored))
        diags.append(diag)
    return finish(member, shares, width), diag_inverse + jnp.stack(diags)


def solution(mesh):
    in_specs = (P("row", "col"), P(None, ("row", "col"), None), P(None, ("row", "col")), P())
    out_specs = (P(("row", "col"), None), P())
    return jax.shard_map(
        per_device, mesh=mesh, in_specs=in_specs, out_specs=out_specs, check_vma=False
    )
```

```python
import functools

import jax
import jax.numpy as jnp
from jax import lax
from jax.experimental import pallas as pl
from jax.experimental.pallas import tpu as pltpu
from jax.sharding import PartitionSpec as P

LANES = 128
BF = jnp.bfloat16
F32 = jnp.float32


def swap(x, axis, bit):
    count = lax.axis_size(axis)
    return lax.ppermute(x, axis, [(i, i ^ bit) for i in range(count)])


def row_bits(row_count):
    return [b for b in (1 << n for n in range(1, 20)) if b < row_count]


def join_kernel(counts, *refs):
    outs = refs[len(refs) - len(counts) :]
    refs = iter(refs)
    for count, out in zip(counts, outs):
        at = 0
        for _ in range(count):
            ref = next(refs)
            out[at : at + ref.shape[0]] = ref[...]
            at += ref.shape[0]


def join(groups, marks=()):
    flat = [x for group in groups for x in group]
    vmem = pl.BlockSpec(memory_space=pltpu.VMEM)
    size = 2 * sum(x.size for x in flat)
    return pl.pallas_call(
        functools.partial(join_kernel, [len(group) for group in groups]),
        in_specs=[vmem] * (len(flat) + len(marks)),
        out_specs=[vmem] * len(groups),
        out_shape=[
            jax.ShapeDtypeStruct((sum(x.shape[0] for x in group), group[0].shape[1]), BF)
            for group in groups
        ],
        compiler_params=pltpu.CompilerParams(vmem_limit_bytes=24 * 2**20),
        cost_estimate=pl.CostEstimate(flops=0, bytes_accessed=2 * size, transcendentals=0),
    )(*flat, *marks)


def gather(owns, marks):
    col_count = lax.axis_size("col")
    bits = row_bits(lax.axis_size("row"))
    half = col_count // 2
    rounds = len(bits) + 1
    state = [None] * len(owns)
    sent = owns[0]
    for tick in range(rounds + len(owns) - 1):
        groups, places = [], []
        for n in range(len(owns)):
            step = tick - n
            if step == 0:
                line = [sent] + [swap(sent, "col", d) for d in range(1, col_count)]
                state[n] = [line[:half], line[half:]]
            elif 0 < step < rounds:
                first, second = state[n]
                state[n] = [
                    [first, swap(first, "row", bits[step - 1])],
                    [second, swap(second, "row", bits[-step])],
                ]
            else:
                continue
            if step == rounds - 1:
                places.append((n, 0))
                groups.append(state[n][0] + state[n][1])
                continue
            for side in range(2):
                places.append((n, side))
                groups.append(state[n][side])
        if tick + 1 < len(owns):
            groups.append([owns[tick + 1]])
        joined = join(groups, tuple(marks[tick : tick + 1]))
        if tick + 1 < len(owns):
            sent = joined[-1]
        for (n, side), value in zip(places, joined):
            state[n][side] = value
        done = tick - rounds + 1
        if done >= 0:
            yield [state[done][0], swap(state[done][0], "row", 1)]


def invert_kernel(listed, sibs, p0, p1, out_ref):
    pieces = (p0, p1)
    lines = out_ref.shape[1]
    count, _, wide = p0.shape
    line_ids = lax.broadcasted_iota(jnp.int32, (lines, wide), 0).astype(F32)
    lane_ids = lax.broadcasted_iota(jnp.int32, (LANES, wide), 0).astype(F32)
    for s in range(sibs):
        total = jnp.zeros((lines, 2 * LANES), F32)
        for n, piece in enumerate(pieces):
            left, right = [], []
            for m in range(count):
                code = piece[m, listed:, :].astype(F32)
                place = 1 + (n * count + m) * listed
                place = place + lax.broadcasted_iota(jnp.int32, (1, wide), 1)
                high = (place // LANES).astype(F32)
                low = (place % LANES).astype(F32)
                left.append(jnp.where(line_ids == code[2 * s : 2 * s + 1], 1.0, 0.0))
                on_lane = lane_ids == code[2 * s + 1 : 2 * s + 2]
                right.append(
                    jnp.concatenate(
                        [jnp.where(on_lane, high, 0.0), jnp.where(on_lane, low, 0.0)], 0
                    )
                )
            total += lax.dot_general(
                jnp.concatenate(left, 1).astype(BF),
                jnp.concatenate(right, 1).astype(BF),
                (((1,), (1,)), ((), ())),
                preferred_element_type=F32,
            )
        out_ref[s] = (total[:, :LANES] * LANES + total[:, LANES:]).astype(jnp.int32)


def invert(pieces, chunk, codes, sibs, rows):
    width = pieces[0].shape[1]
    pieces = [p.reshape(-1, chunk + codes, width) for p in pieces]
    vmem = pl.BlockSpec(memory_space=pltpu.VMEM)
    return pl.pallas_call(
        functools.partial(invert_kernel, chunk, sibs),
        in_specs=[vmem] * 2,
        out_specs=pl.BlockSpec(memory_space=pltpu.VMEM),
        out_shape=jax.ShapeDtypeStruct((sibs, rows // LANES, LANES), jnp.int32),
        compiler_params=pltpu.CompilerParams(vmem_limit_bytes=16 * 2**20),
        cost_estimate=pl.CostEstimate(
            flops=4 * 10**9, bytes_accessed=4 * sibs * rows, transcendentals=0
        ),
    )(*pieces)


def tables_kernel(chunk, row_inv, col_inv, p0, p1, *refs):
    row_out, col_out, mark, source, target = refs[-5:]
    mark[...] = jnp.zeros_like(mark)
    step = 256
    width = col_out.shape[1]
    parts = width // LANES
    count = p0.shape[0]
    source[0 : 8 * parts, :] = jnp.zeros((8 * parts, LANES), F32)
    for n, piece in enumerate((p0, p1)):

        def fill(m, unused, n=n, piece=piece):
            values = piece[m, :chunk, :].astype(F32)
            base = parts * (1 + (n * count + m) * chunk)
            for q in range(parts):
                source[pl.ds(base + q, chunk, stride=parts), :] = values[
                    :, q * LANES : (q + 1) * LANES
                ]
            return unused

        lax.fori_loop(0, count, fill, 0)

    def pick(inv):
        batch = 16

        def line(h, unused):
            for first in range(0, LANES, batch):
                found = [
                    source[pl.ds(pl.multiple_of(parts * inv[h, first + u], parts), parts), :]
                    for u in range(batch)
                ]
                for u in range(batch):
                    target[
                        pl.ds(pl.multiple_of(parts * (h * LANES + first + u), parts), parts), :
                    ] = found[u]
            return unused

        lax.fori_loop(0, inv.shape[0], line, 0)

    pick(row_inv)
    for n in range(row_out.shape[1] // step):
        for q in range(parts):
            values = target[pl.ds(parts * n * step + q, step, stride=parts), :]
            row_out[q * LANES : (q + 1) * LANES, n * step : (n + 1) * step] = values.T.astype(BF)
    pick(col_inv)

    def drain(n, unused):
        at = pl.multiple_of(n * step, step)
        for q in range(parts):
            values = target[pl.ds(parts * at + q, step, stride=parts), :]
            col_out[pl.ds(at, step), q * LANES : (q + 1) * LANES] = values.astype(BF)
        return unused

    lax.fori_loop(0, col_out.shape[0] // step, drain, 0)


def tables(pieces, chunk, whole_chunk, row_inv, col_inv, marks):
    width = pieces[0].shape[1]
    pieces = [p.reshape(-1, whole_chunk, width) for p in pieces]
    count = pieces[0].shape[0]
    listed = 2 * count * chunk
    parts = width // LANES
    rows, cols = row_inv.size, col_inv.size
    vmem = pl.BlockSpec(memory_space=pltpu.VMEM)
    smem = pl.BlockSpec(memory_space=pltpu.SMEM)
    return pl.pallas_call(
        functools.partial(tables_kernel, chunk),
        in_specs=[smem, smem] + [vmem] * (2 + len(marks)),
        out_specs=[vmem] * 3,
        out_shape=[
            jax.ShapeDtypeStruct((width, rows), BF),
            jax.ShapeDtypeStruct((cols, width), BF),
            jax.ShapeDtypeStruct((8, LANES), F32),
        ],
        scratch_shapes=[
            pltpu.VMEM((parts * (listed + 8), LANES), F32),
            pltpu.VMEM((parts * max(rows, cols), LANES), F32),
        ],
        compiler_params=pltpu.CompilerParams(vmem_limit_bytes=28 * 2**20),
        cost_estimate=pl.CostEstimate(
            flops=10**10, bytes_accessed=2 * width * (listed + rows + cols), transcendentals=0
        ),
    )(row_inv, col_inv, *pieces, *marks)


def block_kernel(ancestor, lower, diagonal, mark, held, arrived, left):
    mark[...] = jnp.zeros_like(mark)
    rows, cols = lower.shape
    step = 256
    wide = 512 if cols % 512 == 0 else cols
    row_start = lax.axis_index("row") * rows
    col_start = lax.axis_index("col") * cols
    ins, outs = [], []
    for n in range(0, rows, step):
        here = held.at[n : n + step]
        ins.append(pltpu.make_async_copy(ancestor.at[n : n + step], here, arrived.at[n // step]))
        outs.append(pltpu.make_async_copy(here, lower.at[n : n + step], left.at[n // step]))
    for copy in ins:
        copy.start()
    diagonal[...] = jnp.zeros_like(diagonal)
    for n in range(rows // step):
        ins[n].wait()
        row_first = row_start + n * step
        at = slice(n * step, (n + 1) * step)

        def strip(m, unused, row_first=row_first, at=at):
            first = pl.multiple_of(m * wide, wide)
            over = pl.ds(first, wide)
            col_first = col_start + first
            empty = row_first + step <= col_first

            @pl.when(empty)
            def none():
                held[at, over] = jnp.zeros((step, wide), BF)

            @pl.when(jnp.logical_not(empty) & (row_first < col_first + wide))
            def some():
                row_ids = row_first + lax.broadcasted_iota(jnp.int32, (step, wide), 0)
                col_ids = col_first + lax.broadcasted_iota(jnp.int32, (step, wide), 1)
                values = held[at, over].astype(F32)
                on = jnp.where(col_ids == row_ids, values, 0.0)
                diagonal[at, :] += jnp.sum(on, axis=1, keepdims=True)
                held[at, over] = jnp.where(col_ids < row_ids, values, 0.0).astype(BF)

            return unused

        lax.fori_loop(0, cols // wide, strip, 0)
        outs[n].start()
    for copy in outs:
        copy.wait()


def lower_block(ancestor):
    rows, cols = ancestor.shape
    anywhere = pl.BlockSpec(memory_space=pl.ANY)
    return pl.pallas_call(
        block_kernel,
        in_specs=[anywhere],
        out_specs=[pl.BlockSpec(memory_space=pltpu.HBM)] + [pl.BlockSpec(memory_space=pltpu.VMEM)] * 2,
        out_shape=[
            jax.ShapeDtypeStruct((rows, cols), BF),
            jax.ShapeDtypeStruct((rows, 1), F32),
            jax.ShapeDtypeStruct((8, LANES), F32),
        ],
        scratch_shapes=[
            pltpu.VMEM((rows, cols), BF),
            pltpu.SemaphoreType.DMA((rows // 256,)),
            pltpu.SemaphoreType.DMA((rows // 256,)),
        ],
        compiler_params=pltpu.CompilerParams(vmem_limit_bytes=24 * 2**20),
        cost_estimate=pl.CostEstimate(
            flops=rows * cols, bytes_accessed=4 * rows * cols, transcendentals=0
        ),
    )(ancestor)


def encode(values, lanes):
    high = values.astype(BF)
    low = (values - high.astype(F32)).astype(BF)
    both = jnp.concatenate([high, low], 1)
    return jnp.concatenate([both[:, n : n + lanes] for n in range(0, both.shape[1], lanes)], 0)


def decode(codes, width):
    rows = codes.shape[0] * codes.shape[1] // (2 * width)
    both = jnp.concatenate([codes[n : n + rows] for n in range(0, codes.shape[0], rows)], 1)
    both = both.astype(F32)
    return both[:, :width] + both[:, width:]


def terms_kernel(plan, block, diagonal, row_t, col, *refs):
    m_send, m_keep, direct, total, rounded, y = refs[-6:]
    i = pl.program_id(0)
    steps = pl.num_programs(0)
    rows = block.shape[0]
    owned = m_send.shape[2]
    tile = 2 * owned
    width = row_t.shape[0]
    coded = m_send.shape[1] - width
    core, swapped, offset, chip = [plan[steps + n] for n in range(4)]
    at_tile = pl.ds(pl.multiple_of(plan[i] * tile, tile), tile)
    values = col[at_tile, :]

    def mirrored(out, slot):
        term = jnp.dot(row_t[...], block[...], preferred_element_type=F32).astype(BF)
        out[slot + swapped, coded:, :] = term[:, :owned]
        out[slot + 1 - swapped, coded:, :] = term[:, owned:]

    @pl.when(i < steps // 2)
    def sent():
        mirrored(m_send, 2 * i)

    @pl.when(i >= steps // 2)
    def kept():
        mirrored(m_keep, 2 * i - steps)

    @pl.when(i == 0)
    def first():
        total[...] = jnp.dot(block[...], values, preferred_element_type=F32)

    @pl.when(i > 0)
    def later():
        total[...] += jnp.dot(block[...], values, preferred_element_type=F32)

    @pl.when(i == steps - 1)
    def last():
        cols = col.shape[0]
        for e in range(rows // owned):
            at = slice(e * owned, (e + 1) * owned)
            back = pl.multiple_of(jnp.clip(e * owned + offset, 0, cols - owned), owned)
            own = diagonal[at, :] * col[pl.ds(back, owned), :].astype(F32)
            term = total[at, :]
            rounded[at, :] = (term + 0.5 * own).astype(BF)
            direct[e] = (term + own).astype(BF)
        half = jnp.dot(row_t[...], rounded[...], preferred_element_type=F32)
        y[...] = half + half.T
        slots = m_send.shape[0]
        share = width // (2 * slots)
        for out, side in ((m_send, 1 - core), (m_keep, core)):
            for e in range(slots):
                start = pl.multiple_of((2 * (e ^ chip) + side) * share, share)
                out[e, :coded, :] = encode(y[pl.ds(start, share), :], owned)


def terms(plan, lower, diagonal, row_t, col, owned, marks):
    rows, cols = lower.shape
    width = col.shape[1]
    steps = cols // (2 * owned)
    count = rows // owned
    everything = [
        pl.BlockSpec(x.shape, lambda i, plan, x=x: (0,) * x.ndim) for x in (diagonal, row_t, col)
    ]
    anywhere = pl.BlockSpec(memory_space=pl.ANY)
    d_spec = pl.BlockSpec((count, owned, width), lambda i, plan: (0, 0, 0))
    coded = 2 * width * width // cols
    m_spec = pl.BlockSpec((steps, coded + width, owned), lambda i, plan: (0, 0, 0))
    grid_spec = pltpu.PrefetchScalarGridSpec(
        num_scalar_prefetch=1,
        grid=(steps,),
        in_specs=[pl.BlockSpec((rows, 2 * owned), lambda i, plan: (0, plan[i]))]
        + everything
        + [anywhere] * len(marks),
        out_specs=[m_spec, m_spec, d_spec],
        scratch_shapes=[
            pltpu.VMEM((rows, width), F32),
            pltpu.VMEM((rows, width), BF),
            pltpu.VMEM((width, width), F32),
        ],
    )
    return pl.pallas_call(
        terms_kernel,
        grid_spec=grid_spec,
        out_shape=[
            jax.ShapeDtypeStruct((steps, coded + width, owned), BF),
            jax.ShapeDtypeStruct((steps, coded + width, owned), BF),
            jax.ShapeDtypeStruct((count, owned, width), BF),
        ],
        compiler_params=pltpu.CompilerParams(vmem_limit_bytes=34 * 2**20),
        cost_estimate=pl.CostEstimate(
            flops=5 * rows * cols * width, bytes_accessed=2 * rows * cols, transcendentals=0
        ),
    )(plan, lower, diagonal, row_t, col, *marks)


def tree_sum(values):
    values = [x.astype(F32) for x in values]
    while len(values) > 1:
        values = [a + b for a, b in zip(values[::2], values[1::2])]
    return values[0]


def sums_kernel(width, counts, outs, marks, *refs):
    ins, outs_refs = refs[: len(refs) - len(outs) - marks], refs[len(refs) - len(outs) :]
    groups, at = [], 0
    for count in counts:
        groups.append(ins[at : at + count])
        at += count
    for ref, pieces in zip(outs_refs, outs):
        for place, group, slot, low, high, coded in pieces:
            addends = [x[slot, low:high] for x in groups[group]]
            if ref.dtype == F32 and coded:
                ref[place] = tree_sum([decode(x, ref.shape[2]) for x in addends])
                continue
            if coded:
                total = tree_sum([decode(x[:coded], width) for x in addends])
                ref[place, :coded] = encode(total, ref.shape[2])
            ref[place, coded:] = tree_sum([x[coded:] for x in addends]).astype(ref.dtype)


def sums(groups, outs, width, marks=()):
    flat = [x for group in groups for x in group]
    shapes = []
    for pieces in outs:
        _, group, _, low, high, coded = pieces[0]
        like = groups[group][0]
        rows, lanes, dtype = high - low, like.shape[2], like.dtype
        if coded == rows:
            rows, lanes, dtype = rows * lanes // (2 * width), width, F32
        shapes.append(jax.ShapeDtypeStruct((len(pieces), rows, lanes), dtype))
    vmem = pl.BlockSpec(memory_space=pltpu.VMEM)
    size = sum(x.size for x in flat)
    return pl.pallas_call(
        functools.partial(sums_kernel, width, [len(group) for group in groups], outs, len(marks)),
        in_specs=[vmem] * len(flat) + [pl.BlockSpec(memory_space=pl.ANY)] * len(marks),
        out_specs=[vmem] * len(outs),
        out_shape=shapes,
        compiler_params=pltpu.CompilerParams(vmem_limit_bytes=16 * 2**20),
        cost_estimate=pl.CostEstimate(flops=size, bytes_accessed=3 * size, transcendentals=0),
    )(*flat, *marks)


def mirrored_share(m_send, m_keep, paths, width):
    col_bits = lax.axis_size("col").bit_length() - 1
    rows, owned = m_keep.shape[1:]
    coded = rows - width
    part = width // paths
    cuts = [0] + [coded + part * (path + 1) for path in range(paths)]
    bits = row_bits(lax.axis_size("row"))
    slots = [list(range(len(m_keep))) for _ in range(paths)]
    groups = [(m_keep, swap(m_send, "row", 1))]
    for n in range(col_bits):
        outs = []
        chosen_bits = []
        for path in range(paths):
            place = col_bits - 1 - n if path else n
            chosen_bits.append(bits[place])
            low, high = cuts[path : path + 2]
            group = 0 if n == 0 else path
            if n:
                low, high = 0, high - low
            codes = 0 if path else coded
            for send in (True, False):
                chosen = [i for i, e in enumerate(slots[path]) if bool(e >> place & 1) == send]
                outs.append([(p, group, i, low, high, codes) for p, i in enumerate(chosen)])
            slots[path] = [e for e in slots[path] if not e >> place & 1]
        made = yield groups, outs
        groups = [
            (made[2 * path + 1], swap(made[2 * path], "row", chosen_bits[path]))
            for path in range(paths)
        ]
    own = []
    for path in range(paths):
        first = 0 if path else coded
        own.append((path, path, 0, first, first + part, 0))
    own, y = yield groups, [own, [(0, 0, 0, 0, coded, coded)]]
    return to_owner(own.reshape(width, owned)), y


def diagonal_sum(ys):
    y = jnp.concatenate(ys, 0)
    bit = 1
    while bit < lax.axis_size("col"):
        y = y + swap(y, "col", bit)
        bit *= 2
    y = y[:, None]
    bit = lax.axis_size("row") // 2
    while bit:
        other = swap(y, "row", bit)
        low = (lax.axis_index("row") & bit) == 0
        both = [jnp.where(low, y, other), jnp.where(low, other, y)]
        y = jnp.stack(both, 2).reshape(y.shape[0], -1, *y.shape[2:])
        bit //= 2
    return y.reshape(y.shape[0], -1, y.shape[3])


class Rounds:
    def __init__(self, width, *chains):
        self.width = width
        self.chains = chains
        self.results = [None] * len(chains)
        self.jobs = {}
        for n, chain in enumerate(chains):
            self.send(n, None)

    def send(self, n, values):
        try:
            self.jobs[n] = self.chains[n].send(values)
        except StopIteration as end:
            self.jobs.pop(n, None)
            self.results[n] = end.value

    def advance(self, *marks):
        groups, outs = [], []
        for job_groups, job_outs in self.jobs.values():
            for pieces in job_outs:
                outs.append([(p, group + len(groups), *rest) for p, group, *rest in pieces])
            groups += job_groups
        made = sums(groups, outs, self.width, marks)
        at = 0
        for n, (_, job_outs) in list(self.jobs.items()):
            self.send(n, made[at : at + len(job_outs)])
            at += len(job_outs)
        return made[-1]

    def finish(self):
        while self.jobs:
            self.advance()
        return self.results


def reversed_bits(value, bits):
    return sum(((value >> n) & 1) << (bits - 1 - n) for n in range(bits))


def to_owner(x):
    row_count = lax.axis_size("row")
    col_count = lax.axis_size("col")
    bits = col_count.bit_length() - 1
    pairs = []
    for row in range(row_count):
        for col in range(col_count):
            place = (row // 2) ^ reversed_bits(col, bits)
            pairs.append((row * col_count + col, (2 * col + row % 2) * col_count + place))
    return lax.ppermute(x, ("row", "col"), pairs)


def finish_kernel(member, *refs):
    out = refs[-1]
    owned = out.shape[0]
    sibs = member.shape[0]
    width = out.shape[1] // sibs
    s = 0
    for n in range(0, len(refs) - 1, 2):
        parts, mirrored = refs[n : n + 2]
        for at in range(0, mirrored.shape[0], width):
            over = slice(at, at + width)
            product = mirrored[over, :].astype(F32).T
            for m in range(parts.shape[0]):
                product = product + parts[m, :, over].astype(F32)
            listed = jnp.broadcast_to(member[s : s + 1, :].astype(F32), (LANES, owned)).T
            for q in range(0, width, LANES):
                out[:, s * width + q : s * width + q + LANES] = jnp.where(
                    listed > 0.5, -product[:, q : q + LANES], 0.0
                ).astype(BF)
            s += 1


def finish(member, shares, width):
    sibs, owned = member.shape
    vmem = pl.BlockSpec(memory_space=pltpu.VMEM)
    flat = [x for share in shares for x in share]
    return pl.pallas_call(
        finish_kernel,
        in_specs=[vmem] * (1 + len(flat)),
        out_specs=vmem,
        out_shape=jax.ShapeDtypeStruct((owned, sibs * width), BF),
        compiler_params=pltpu.CompilerParams(vmem_limit_bytes=24 * 2**20),
        cost_estimate=pl.CostEstimate(
            flops=4 * owned * sibs * width,
            bytes_accessed=8 * owned * sibs * width,
            transcendentals=0,
        ),
    )(member, *flat)


def per_device(ancestor, panels, row_index, diag_inverse):
    row_count = lax.axis_size("row")
    col_count = lax.axis_size("col")
    assert row_count == 2 * col_count
    block_rows, block_cols = ancestor.shape
    sib_count, listed, width = panels.shape
    owned = block_rows // col_count
    row_place = lax.axis_index("row")
    col_place = lax.axis_index("col")
    core = row_place % 2
    chip = row_place // 2
    col_bits = col_count.bit_length() - 1
    row_lines, col_lines, own_lines = block_rows // LANES, block_cols // LANES, owned // LANES
    mixed = chip ^ sum(((col_place >> n) & 1) << (col_bits - 1 - n) for n in range(col_bits))
    pairs = [(2 * n ^ mixed) // 2 for n in range(col_count // 2)]
    plan = jnp.stack(
        [n + (1 - core) * (col_count // 2) for n in pairs]
        + [n + core * (col_count // 2) for n in pairs]
        + [core, mixed % 2, row_place * block_rows - col_place * block_cols, chip]
    ).astype(jnp.int32)

    codes = jnp.stack([row_index // LANES, row_index % LANES], 1).astype(BF)
    codes = codes.reshape(-1, listed)
    code_rows = -(-len(codes) // 16) * 16
    codes = jnp.pad(
        codes, ((0, code_rows - len(codes)), (0, width - listed)), constant_values=-1
    )
    owns = [jnp.concatenate([panels[0], codes], 0)] + [panels[s] for s in range(1, sib_count)]
    chunks = [listed + code_rows] + [listed] * (sib_count - 1)

    lower, diagonal, mark = lower_block(ancestor)
    marks = [mark] * (len(row_bits(row_count)) + 1)
    gathered = gather(owns, marks)
    both, direct = [], []
    row_inv = col_inv = member = None
    for s in range(sib_count):
        pieces = next(gathered)
        if s == 0:
            inverse = invert(pieces, listed, code_rows, sib_count, block_rows * row_count)
            row_inv = lax.dynamic_slice_in_dim(inverse, row_place * row_lines, row_lines, 1)
            col_inv = lax.dynamic_slice_in_dim(inverse, col_place * col_lines, col_lines, 1)
            own_inv = lax.dynamic_slice_in_dim(
                inverse, row_place * row_lines + col_place * own_lines, own_lines, 1
            )
            member = own_inv.reshape(sib_count, owned)
        before = [chain.advance() for chain in both[-1:]] + direct[:-1]
        row_t, col, mark = tables(pieces, listed, chunks[s], row_inv[s], col_inv[s], before)
        marks.append(mark)
        before = [chain.advance(mark) for chain in both if chain.jobs]
        m_send, m_keep, parts = terms(plan, lower, diagonal, row_t, col, owned, before)
        paths = 2 if s == sib_count - 1 else 1
        both.append(Rounds(width, mirrored_share(m_send, m_keep, paths, width)))
        direct.append(lax.all_to_all(parts, "col", 0, 0, tiled=True))
    both[-1].advance(*direct[-2:-1])
    mark = both[-1].advance()
    for chain in both[:-1]:
        while chain.jobs:
            chain.advance(mark)
    while both[-1].jobs:
        both[-1].advance(*direct[-1:])
    shares, ys = [], []
    for s in range(sib_count):
        mirrored, y = both[s].results[0]
        shares.append((direct[s], mirrored))
        ys.append(y)
    diags = jnp.concatenate([diagonal_sum(ys[:-1]), diagonal_sum(ys[-1:])], 0)
    return finish(member, shares, width), diag_inverse + diags


def solution(mesh):
    in_specs = (P("row", "col"), P(None, ("row", "col"), None), P(None, ("row", "col")), P())
    out_specs = (P(("row", "col"), None), P())
    return jax.shard_map(
        per_device, mesh=mesh, in_specs=in_specs, out_specs=out_specs, check_vma=False
    )
```

```python
import functools

import jax
import jax.numpy as jnp
from jax import lax
from jax.experimental import pallas as pl
from jax.experimental.pallas import tpu as pltpu
from jax.sharding import PartitionSpec as P

LANES = 128
BF = jnp.bfloat16
F32 = jnp.float32


def swap(x, axis, bit):
    count = lax.axis_size(axis)
    return lax.ppermute(x, axis, [(i, i ^ bit) for i in range(count)])


def row_bits(row_count):
    return [b for b in (1 << n for n in range(1, 20)) if b < row_count]


def join_kernel(counts, *refs):
    outs = refs[len(refs) - len(counts) :]
    refs = iter(refs)
    for count, out in zip(counts, outs):
        at = 0
        for _ in range(count):
            ref = next(refs)
            out[at : at + ref.shape[0]] = ref[...]
            at += ref.shape[0]


def join(groups, marks=()):
    flat = [x for group in groups for x in group]
    vmem = pl.BlockSpec(memory_space=pltpu.VMEM)
    size = 2 * sum(x.size for x in flat)
    return pl.pallas_call(
        functools.partial(join_kernel, [len(group) for group in groups]),
        in_specs=[vmem] * (len(flat) + len(marks)),
        out_specs=[vmem] * len(groups),
        out_shape=[
            jax.ShapeDtypeStruct((sum(x.shape[0] for x in group), group[0].shape[1]), BF)
            for group in groups
        ],
        compiler_params=pltpu.CompilerParams(vmem_limit_bytes=24 * 2**20),
        cost_estimate=pl.CostEstimate(flops=0, bytes_accessed=2 * size, transcendentals=0),
    )(*flat, *marks)


def gather(owns, marks):
    col_count = lax.axis_size("col")
    bits = row_bits(lax.axis_size("row"))
    half = col_count // 2
    rounds = len(bits) + 1
    state = [None] * len(owns)
    sent = owns[0]
    for tick in range(rounds + len(owns) - 1):
        groups, places = [], []
        for n in range(len(owns)):
            step = tick - n
            if step == 0:
                line = [sent] + [swap(sent, "col", d) for d in range(1, col_count)]
                state[n] = [line[:half], line[half:]]
            elif 0 < step < rounds:
                first, second = state[n]
                state[n] = [
                    [first, swap(first, "row", bits[step - 1])],
                    [second, swap(second, "row", bits[-step])],
                ]
            else:
                continue
            if step == rounds - 1:
                places.append((n, 0))
                groups.append(state[n][0] + state[n][1])
                continue
            for side in range(2):
                places.append((n, side))
                groups.append(state[n][side])
        if tick + 1 < len(owns):
            groups.append([owns[tick + 1]])
        joined = join(groups, tuple(marks[tick : tick + 1]))
        if tick + 1 < len(owns):
            sent = joined[-1]
        for (n, side), value in zip(places, joined):
            state[n][side] = value
        done = tick - rounds + 1
        if done >= 0:
            yield [state[done][0], swap(state[done][0], "row", 1)]


def invert_kernel(listed, lists, p0, p1, *refs):
    out_ref = refs[-1]
    pieces = (p0, p1)
    lines = out_ref.shape[1]
    count, _, wide = p0.shape
    line_ids = lax.broadcasted_iota(jnp.int32, (lines, wide), 0).astype(F32)
    lane_ids = lax.broadcasted_iota(jnp.int32, (LANES, wide), 0).astype(F32)
    for at, s in enumerate(lists):
        total = jnp.zeros((lines, 2 * LANES), F32)
        for n, piece in enumerate(pieces):
            left, right = [], []
            for m in range(count):
                code = piece[m, listed:, :].astype(F32)
                place = 1 + (n * count + m) * listed
                place = place + lax.broadcasted_iota(jnp.int32, (1, wide), 1)
                high = (place // LANES).astype(F32)
                low = (place % LANES).astype(F32)
                left.append(jnp.where(line_ids == code[2 * s : 2 * s + 1], 1.0, 0.0))
                on_lane = lane_ids == code[2 * s + 1 : 2 * s + 2]
                right.append(
                    jnp.concatenate(
                        [jnp.where(on_lane, high, 0.0), jnp.where(on_lane, low, 0.0)], 0
                    )
                )
            total += lax.dot_general(
                jnp.concatenate(left, 1).astype(BF),
                jnp.concatenate(right, 1).astype(BF),
                (((1,), (1,)), ((), ())),
                preferred_element_type=F32,
            )
        out_ref[at] = (total[:, :LANES] * LANES + total[:, LANES:]).astype(jnp.int32)


def invert(pieces, chunk, codes, lists, rows, marks):
    width = pieces[0].shape[1]
    pieces = [p.reshape(-1, chunk + codes, width) for p in pieces]
    vmem = pl.BlockSpec(memory_space=pltpu.VMEM)
    return pl.pallas_call(
        functools.partial(invert_kernel, chunk, lists),
        in_specs=[vmem] * 2 + [pl.BlockSpec(memory_space=pl.ANY)] * len(marks),
        out_specs=pl.BlockSpec(memory_space=pltpu.VMEM),
        out_shape=jax.ShapeDtypeStruct((len(lists), rows // LANES, LANES), jnp.int32),
        compiler_params=pltpu.CompilerParams(vmem_limit_bytes=16 * 2**20),
        cost_estimate=pl.CostEstimate(
            flops=10**9 * len(lists), bytes_accessed=4 * len(lists) * rows, transcendentals=0
        ),
    )(*pieces, *marks)


def tables_kernel(chunk, row_inv, col_inv, p0, p1, *refs):
    row_out, col_out, mark, source, target = refs[-5:]
    mark[...] = jnp.zeros_like(mark)
    step = 256
    width = col_out.shape[1]
    parts = width // LANES
    count = p0.shape[0]
    source[0 : 8 * parts, :] = jnp.zeros((8 * parts, LANES), F32)
    for n, piece in enumerate((p0, p1)):

        def fill(m, unused, n=n, piece=piece):
            values = piece[m, :chunk, :].astype(F32)
            base = parts * (1 + (n * count + m) * chunk)
            for q in range(parts):
                source[pl.ds(base + q, chunk, stride=parts), :] = values[
                    :, q * LANES : (q + 1) * LANES
                ]
            return unused

        lax.fori_loop(0, count, fill, 0)

    def pick(inv):
        batch = 16

        def line(h, unused):
            for first in range(0, LANES, batch):
                found = [
                    source[pl.ds(pl.multiple_of(parts * inv[h, first + u], parts), parts), :]
                    for u in range(batch)
                ]
                for u in range(batch):
                    target[
                        pl.ds(pl.multiple_of(parts * (h * LANES + first + u), parts), parts), :
                    ] = found[u]
            return unused

        lax.fori_loop(0, inv.shape[0], line, 0)

    pick(row_inv)
    for n in range(row_out.shape[1] // step):
        for q in range(parts):
            values = target[pl.ds(parts * n * step + q, step, stride=parts), :]
            row_out[q * LANES : (q + 1) * LANES, n * step : (n + 1) * step] = values.T.astype(BF)
    pick(col_inv)

    def drain(n, unused):
        at = pl.multiple_of(n * step, step)
        for q in range(parts):
            values = target[pl.ds(parts * at + q, step, stride=parts), :]
            col_out[pl.ds(at, step), q * LANES : (q + 1) * LANES] = values.astype(BF)
        return unused

    lax.fori_loop(0, col_out.shape[0] // step, drain, 0)


def tables(pieces, chunk, whole_chunk, row_inv, col_inv, marks):
    width = pieces[0].shape[1]
    pieces = [p.reshape(-1, whole_chunk, width) for p in pieces]
    count = pieces[0].shape[0]
    listed = 2 * count * chunk
    parts = width // LANES
    rows, cols = row_inv.size, col_inv.size
    vmem = pl.BlockSpec(memory_space=pltpu.VMEM)
    smem = pl.BlockSpec(memory_space=pltpu.SMEM)
    return pl.pallas_call(
        functools.partial(tables_kernel, chunk),
        in_specs=[smem, smem] + [vmem] * (2 + len(marks)),
        out_specs=[vmem] * 3,
        out_shape=[
            jax.ShapeDtypeStruct((width, rows), BF),
            jax.ShapeDtypeStruct((cols, width), BF),
            jax.ShapeDtypeStruct((8, LANES), F32),
        ],
        scratch_shapes=[
            pltpu.VMEM((parts * (listed + 8), LANES), F32),
            pltpu.VMEM((parts * max(rows, cols), LANES), F32),
        ],
        compiler_params=pltpu.CompilerParams(vmem_limit_bytes=28 * 2**20),
        cost_estimate=pl.CostEstimate(
            flops=10**10, bytes_accessed=2 * width * (listed + rows + cols), transcendentals=0
        ),
    )(row_inv, col_inv, *pieces, *marks)


def block_kernel(ancestor, lower, diagonal, mark, held, arrived, left):
    mark[...] = jnp.zeros_like(mark)
    rows, cols = lower.shape
    step = 256
    wide = 512 if cols % 512 == 0 else cols
    row_start = lax.axis_index("row") * rows
    col_start = lax.axis_index("col") * cols
    ins, outs = [], []
    for n in range(0, rows, step):
        here = held.at[n : n + step]
        ins.append(pltpu.make_async_copy(ancestor.at[n : n + step], here, arrived.at[n // step]))
        outs.append(pltpu.make_async_copy(here, lower.at[n : n + step], left.at[n // step]))
    for copy in ins:
        copy.start()
    diagonal[...] = jnp.zeros_like(diagonal)
    for n in range(rows // step):
        ins[n].wait()
        row_first = row_start + n * step
        at = slice(n * step, (n + 1) * step)

        def strip(m, unused, row_first=row_first, at=at):
            first = pl.multiple_of(m * wide, wide)
            over = pl.ds(first, wide)
            col_first = col_start + first
            empty = row_first + step <= col_first

            @pl.when(empty)
            def none():
                held[at, over] = jnp.zeros((step, wide), BF)

            @pl.when(jnp.logical_not(empty) & (row_first < col_first + wide))
            def some():
                row_ids = row_first + lax.broadcasted_iota(jnp.int32, (step, wide), 0)
                col_ids = col_first + lax.broadcasted_iota(jnp.int32, (step, wide), 1)
                values = held[at, over].astype(F32)
                on = jnp.where(col_ids == row_ids, values, 0.0)
                diagonal[at, :] += jnp.sum(on, axis=1, keepdims=True)
                held[at, over] = jnp.where(col_ids < row_ids, values, 0.0).astype(BF)

            return unused

        lax.fori_loop(0, cols // wide, strip, 0)
        outs[n].start()
    for copy in outs:
        copy.wait()


def lower_block(ancestor):
    rows, cols = ancestor.shape
    anywhere = pl.BlockSpec(memory_space=pl.ANY)
    return pl.pallas_call(
        block_kernel,
        in_specs=[anywhere],
        out_specs=[pl.BlockSpec(memory_space=pltpu.HBM)] + [pl.BlockSpec(memory_space=pltpu.VMEM)] * 2,
        out_shape=[
            jax.ShapeDtypeStruct((rows, cols), BF),
            jax.ShapeDtypeStruct((rows, 1), F32),
            jax.ShapeDtypeStruct((8, LANES), F32),
        ],
        scratch_shapes=[
            pltpu.VMEM((rows, cols), BF),
            pltpu.SemaphoreType.DMA((rows // 256,)),
            pltpu.SemaphoreType.DMA((rows // 256,)),
        ],
        compiler_params=pltpu.CompilerParams(vmem_limit_bytes=24 * 2**20),
        cost_estimate=pl.CostEstimate(
            flops=rows * cols, bytes_accessed=4 * rows * cols, transcendentals=0
        ),
    )(ancestor)


def encode(values, lanes):
    high = values.astype(BF)
    low = (values - high.astype(F32)).astype(BF)
    both = jnp.concatenate([high, low], 1)
    return jnp.concatenate([both[:, n : n + lanes] for n in range(0, both.shape[1], lanes)], 0)


def decode(codes, width):
    rows = codes.shape[0] * codes.shape[1] // (2 * width)
    both = jnp.concatenate([codes[n : n + rows] for n in range(0, codes.shape[0], rows)], 1)
    both = both.astype(F32)
    return both[:, :width] + both[:, width:]


def terms_kernel(plan, block, diagonal, row_t, col, *refs):
    m_send, m_keep, direct, total, rounded, y = refs[-6:]
    i = pl.program_id(0)
    steps = pl.num_programs(0)
    rows = block.shape[0]
    owned = m_send.shape[2]
    tile = 2 * owned
    width = row_t.shape[0]
    coded = m_send.shape[1] - width
    core, swapped, offset, chip = [plan[steps + n] for n in range(4)]
    at_tile = pl.ds(pl.multiple_of(plan[i] * tile, tile), tile)
    values = col[at_tile, :]

    def mirrored(out, slot):
        term = jnp.dot(row_t[...], block[...], preferred_element_type=F32).astype(BF)
        out[slot + swapped, coded:, :] = term[:, :owned]
        out[slot + 1 - swapped, coded:, :] = term[:, owned:]

    @pl.when(i < steps // 2)
    def sent():
        mirrored(m_send, 2 * i)

    @pl.when(i >= steps // 2)
    def kept():
        mirrored(m_keep, 2 * i - steps)

    @pl.when(i == 0)
    def first():
        total[...] = jnp.dot(block[...], values, preferred_element_type=F32)

    @pl.when(i > 0)
    def later():
        total[...] += jnp.dot(block[...], values, preferred_element_type=F32)

    @pl.when(i == steps - 1)
    def last():
        cols = col.shape[0]
        for e in range(rows // owned):
            at = slice(e * owned, (e + 1) * owned)
            back = pl.multiple_of(jnp.clip(e * owned + offset, 0, cols - owned), owned)
            own = diagonal[at, :] * col[pl.ds(back, owned), :].astype(F32)
            term = total[at, :]
            rounded[at, :] = (term + 0.5 * own).astype(BF)
            direct[e] = (term + own).astype(BF)
        half = jnp.dot(row_t[...], rounded[...], preferred_element_type=F32)
        y[...] = half + half.T
        slots = m_send.shape[0]
        share = width // (2 * slots)
        for out, side in ((m_send, 1 - core), (m_keep, core)):
            for e in range(slots):
                start = pl.multiple_of((2 * (e ^ chip) + side) * share, share)
                out[e, :coded, :] = encode(y[pl.ds(start, share), :], owned)


def terms(plan, lower, diagonal, row_t, col, owned, marks):
    rows, cols = lower.shape
    width = col.shape[1]
    steps = cols // (2 * owned)
    count = rows // owned
    everything = [
        pl.BlockSpec(x.shape, lambda i, plan, x=x: (0,) * x.ndim) for x in (diagonal, row_t, col)
    ]
    anywhere = pl.BlockSpec(memory_space=pl.ANY)
    d_spec = pl.BlockSpec((count, owned, width), lambda i, plan: (0, 0, 0))
    coded = 2 * width * width // cols
    m_spec = pl.BlockSpec((steps, coded + width, owned), lambda i, plan: (0, 0, 0))
    grid_spec = pltpu.PrefetchScalarGridSpec(
        num_scalar_prefetch=1,
        grid=(steps,),
        in_specs=[pl.BlockSpec((rows, 2 * owned), lambda i, plan: (0, plan[i]))]
        + everything
        + [anywhere] * len(marks),
        out_specs=[m_spec, m_spec, d_spec],
        scratch_shapes=[
            pltpu.VMEM((rows, width), F32),
            pltpu.VMEM((rows, width), BF),
            pltpu.VMEM((width, width), F32),
        ],
    )
    return pl.pallas_call(
        terms_kernel,
        grid_spec=grid_spec,
        out_shape=[
            jax.ShapeDtypeStruct((steps, coded + width, owned), BF),
            jax.ShapeDtypeStruct((steps, coded + width, owned), BF),
            jax.ShapeDtypeStruct((count, owned, width), BF),
        ],
        compiler_params=pltpu.CompilerParams(vmem_limit_bytes=34 * 2**20),
        cost_estimate=pl.CostEstimate(
            flops=5 * rows * cols * width, bytes_accessed=2 * rows * cols, transcendentals=0
        ),
    )(plan, lower, diagonal, row_t, col, *marks)


def tree_sum(values):
    values = [x.astype(F32) for x in values]
    while len(values) > 1:
        values = [a + b for a, b in zip(values[::2], values[1::2])]
    return values[0]


def sums_kernel(width, counts, outs, marks, *refs):
    ins, outs_refs = refs[: len(refs) - len(outs) - marks], refs[len(refs) - len(outs) :]
    groups, at = [], 0
    for count in counts:
        groups.append(ins[at : at + count])
        at += count
    for ref, pieces in zip(outs_refs, outs):
        for place, group, slot, low, high, coded in pieces:
            addends = [x[slot, low:high] for x in groups[group]]
            if ref.dtype == F32 and coded:
                ref[place] = tree_sum([decode(x, ref.shape[2]) for x in addends])
                continue
            if coded:
                total = tree_sum([decode(x[:coded], width) for x in addends])
                ref[place, :coded] = encode(total, ref.shape[2])
            ref[place, coded:] = tree_sum([x[coded:] for x in addends]).astype(ref.dtype)


def sums(groups, outs, width, marks=()):
    flat = [x for group in groups for x in group]
    shapes = []
    for pieces in outs:
        _, group, _, low, high, coded = pieces[0]
        like = groups[group][0]
        rows, lanes, dtype = high - low, like.shape[2], like.dtype
        if coded == rows:
            rows, lanes, dtype = rows * lanes // (2 * width), width, F32
        shapes.append(jax.ShapeDtypeStruct((len(pieces), rows, lanes), dtype))
    vmem = pl.BlockSpec(memory_space=pltpu.VMEM)
    size = sum(x.size for x in flat)
    return pl.pallas_call(
        functools.partial(sums_kernel, width, [len(group) for group in groups], outs, len(marks)),
        in_specs=[vmem] * len(flat) + [pl.BlockSpec(memory_space=pl.ANY)] * len(marks),
        out_specs=[vmem] * len(outs),
        out_shape=shapes,
        compiler_params=pltpu.CompilerParams(vmem_limit_bytes=16 * 2**20),
        cost_estimate=pl.CostEstimate(flops=size, bytes_accessed=3 * size, transcendentals=0),
    )(*flat, *marks)


def mirrored_share(m_send, m_keep, paths, width):
    col_bits = lax.axis_size("col").bit_length() - 1
    rows, owned = m_keep.shape[1:]
    coded = rows - width
    part = width // paths
    cuts = [0] + [coded + part * (path + 1) for path in range(paths)]
    bits = row_bits(lax.axis_size("row"))
    slots = [list(range(len(m_keep))) for _ in range(paths)]
    groups = [(m_keep, swap(m_send, "row", 1))]
    for n in range(col_bits):
        outs = []
        chosen_bits = []
        for path in range(paths):
            place = col_bits - 1 - n if path else n
            chosen_bits.append(bits[place])
            low, high = cuts[path : path + 2]
            group = 0 if n == 0 else path
            if n:
                low, high = 0, high - low
            codes = 0 if path else coded
            for send in (True, False):
                chosen = [i for i, e in enumerate(slots[path]) if bool(e >> place & 1) == send]
                outs.append([(p, group, i, low, high, codes) for p, i in enumerate(chosen)])
            slots[path] = [e for e in slots[path] if not e >> place & 1]
        made = yield groups, outs
        groups = [
            (made[2 * path + 1], swap(made[2 * path], "row", chosen_bits[path]))
            for path in range(paths)
        ]
    own = []
    for path in range(paths):
        first = 0 if path else coded
        own.append((path, path, 0, first, first + part, 0))
    own, y = yield groups, [own, [(0, 0, 0, 0, coded, coded)]]
    return to_owner(own.reshape(width, owned)), y


def diagonal_sum(ys, early):
    y = jnp.concatenate(ys, 0)[:, None]
    bits = []
    bit = lax.axis_size("row") // 2
    while bit:
        bits.append(bit)
        bit //= 2
    for n, bit in enumerate(bits):
        if n == (0 if early else len(bits) - 1):
            along = 1
            while along < lax.axis_size("col"):
                y = y + swap(y, "col", along)
                along *= 2
        other = swap(y, "row", bit)
        low = (lax.axis_index("row") & bit) == 0
        both = [jnp.where(low, y, other), jnp.where(low, other, y)]
        y = jnp.stack(both, 2).reshape(y.shape[0], -1, *y.shape[2:])
    return y.reshape(y.shape[0], -1, y.shape[3])


class Rounds:
    def __init__(self, width, *chains):
        self.width = width
        self.chains = chains
        self.results = [None] * len(chains)
        self.jobs = {}
        for n, chain in enumerate(chains):
            self.send(n, None)

    def send(self, n, values):
        try:
            self.jobs[n] = self.chains[n].send(values)
        except StopIteration as end:
            self.jobs.pop(n, None)
            self.results[n] = end.value

    def advance(self, *marks):
        groups, outs = [], []
        for job_groups, job_outs in self.jobs.values():
            for pieces in job_outs:
                outs.append([(p, group + len(groups), *rest) for p, group, *rest in pieces])
            groups += job_groups
        made = sums(groups, outs, self.width, marks)
        at = 0
        for n, (_, job_outs) in list(self.jobs.items()):
            self.send(n, made[at : at + len(job_outs)])
            at += len(job_outs)
        return made[-1]

    def finish(self):
        while self.jobs:
            self.advance()
        return self.results


def reversed_bits(value, bits):
    return sum(((value >> n) & 1) << (bits - 1 - n) for n in range(bits))


def to_owner(x):
    row_count = lax.axis_size("row")
    col_count = lax.axis_size("col")
    bits = col_count.bit_length() - 1
    pairs = []
    for row in range(row_count):
        for col in range(col_count):
            place = (row // 2) ^ reversed_bits(col, bits)
            pairs.append((row * col_count + col, (2 * col + row % 2) * col_count + place))
    return lax.ppermute(x, ("row", "col"), pairs)


def finish_kernel(member, *refs):
    out = refs[-1]
    owned = out.shape[0]
    sibs = member.shape[0]
    width = out.shape[1] // sibs
    s = 0
    for n in range(0, len(refs) - 1, 2):
        parts, mirrored = refs[n : n + 2]
        for at in range(0, mirrored.shape[0], width):
            over = slice(at, at + width)
            product = mirrored[over, :].astype(F32).T
            for m in range(parts.shape[0]):
                product = product + parts[m, :, over].astype(F32)
            listed = jnp.broadcast_to(member[s : s + 1, :].astype(F32), (LANES, owned)).T
            for q in range(0, width, LANES):
                out[:, s * width + q : s * width + q + LANES] = jnp.where(
                    listed > 0.5, -product[:, q : q + LANES], 0.0
                ).astype(BF)
            s += 1


def finish(member, shares, width):
    sibs, owned = member.shape
    vmem = pl.BlockSpec(memory_space=pltpu.VMEM)
    flat = [x for share in shares for x in share]
    return pl.pallas_call(
        finish_kernel,
        in_specs=[vmem] * (1 + len(flat)),
        out_specs=vmem,
        out_shape=jax.ShapeDtypeStruct((owned, sibs * width), BF),
        compiler_params=pltpu.CompilerParams(vmem_limit_bytes=24 * 2**20),
        cost_estimate=pl.CostEstimate(
            flops=4 * owned * sibs * width,
            bytes_accessed=8 * owned * sibs * width,
            transcendentals=0,
        ),
    )(member, *flat)


def per_device(ancestor, panels, row_index, diag_inverse):
    row_count = lax.axis_size("row")
    col_count = lax.axis_size("col")
    assert row_count == 2 * col_count
    block_rows, block_cols = ancestor.shape
    sib_count, listed, width = panels.shape
    owned = block_rows // col_count
    row_place = lax.axis_index("row")
    col_place = lax.axis_index("col")
    core = row_place % 2
    chip = row_place // 2
    col_bits = col_count.bit_length() - 1
    row_lines, col_lines, own_lines = block_rows // LANES, block_cols // LANES, owned // LANES
    mixed = chip ^ sum(((col_place >> n) & 1) << (col_bits - 1 - n) for n in range(col_bits))
    pairs = [(2 * n ^ mixed) // 2 for n in range(col_count // 2)]
    plan = jnp.stack(
        [n + (1 - core) * (col_count // 2) for n in pairs]
        + [n + core * (col_count // 2) for n in pairs]
        + [core, mixed % 2, row_place * block_rows - col_place * block_cols, chip]
    ).astype(jnp.int32)

    codes = jnp.stack([row_index // LANES, row_index % LANES], 1).astype(BF)
    codes = codes.reshape(-1, listed)
    code_rows = -(-len(codes) // 16) * 16
    codes = jnp.pad(
        codes, ((0, code_rows - len(codes)), (0, width - listed)), constant_values=-1
    )
    owns = [jnp.concatenate([panels[0], codes], 0)] + [panels[s] for s in range(1, sib_count)]
    chunks = [listed + code_rows] + [listed] * (sib_count - 1)

    lower, diagonal, mark = lower_block(ancestor)
    marks = [mark] * (len(row_bits(row_count)) + 1)
    gathered = gather(owns, marks)
    both, direct = [], []
    row_inv = col_inv = None
    members = []
    for s in range(sib_count):
        pieces = next(gathered)
        if s == 0:
            coded = pieces
            inverse = invert(coded, listed, code_rows, [0], block_rows * row_count, [])
        elif s == 1:
            rest = list(range(1, sib_count))
            inverse = invert(coded, listed, code_rows, rest, block_rows * row_count, [mark])
        if s < 2:
            row_inv = lax.dynamic_slice_in_dim(inverse, row_place * row_lines, row_lines, 1)
            col_inv = lax.dynamic_slice_in_dim(inverse, col_place * col_lines, col_lines, 1)
            own_inv = lax.dynamic_slice_in_dim(
                inverse, row_place * row_lines + col_place * own_lines, own_lines, 1
            )
            members.append(own_inv.reshape(-1, owned))
        at = max(s - 1, 0)
        before = [chain.advance() for chain in both if chain.jobs] + direct[:-1]
        row_t, col, mark = tables(pieces, listed, chunks[s], row_inv[at], col_inv[at], before)
        marks.append(mark)
        before = [chain.advance(mark) for chain in both[-1:] if chain.jobs]
        before += [chain.results[0][0] for chain in both if not chain.jobs]
        m_send, m_keep, parts = terms(plan, lower, diagonal, row_t, col, owned, before)
        paths = 2
        both.append(Rounds(width, mirrored_share(m_send, m_keep, paths, width)))
        direct.append(lax.all_to_all(parts, "col", 0, 0, tiled=True))
    both[-1].advance(*direct[-2:-1])
    mark = both[-1].advance()
    for chain in both[:-1]:
        while chain.jobs:
            chain.advance(mark)
    while both[-1].jobs:
        both[-1].advance(*direct[-1:])
    shares, ys = [], []
    for s in range(sib_count):
        mirrored, y = both[s].results[0]
        shares.append((direct[s], mirrored))
        ys.append(y)
    diags = jnp.concatenate([diagonal_sum(ys[:-1], True), diagonal_sum(ys[-1:], False)], 0)
    return finish(jnp.concatenate(members, 0), shares, width), diag_inverse + diags


def solution(mesh):
    in_specs = (P("row", "col"), P(None, ("row", "col"), None), P(None, ("row", "col")), P())
    out_specs = (P(("row", "col"), None), P())
    return jax.shard_map(
        per_device, mesh=mesh, in_specs=in_specs, out_specs=out_specs, check_vma=False
    )
```

```python
import functools

import jax
import jax.numpy as jnp
from jax import lax
from jax.experimental import pallas as pl
from jax.experimental.pallas import tpu as pltpu
from jax.sharding import PartitionSpec as P

LANES = 128
BF = jnp.bfloat16
F32 = jnp.float32


def swap(x, axis, bit):
    count = lax.axis_size(axis)
    return lax.ppermute(x, axis, [(i, i ^ bit) for i in range(count)])


def row_bits(row_count):
    return [b for b in (1 << n for n in range(1, 20)) if b < row_count]


def join_kernel(counts, *refs):
    outs = refs[len(refs) - len(counts) :]
    refs = iter(refs)
    for count, out in zip(counts, outs):
        at = 0
        for _ in range(count):
            ref = next(refs)
            out[at : at + ref.shape[0]] = ref[...]
            at += ref.shape[0]


def join(groups, marks=()):
    flat = [x for group in groups for x in group]
    vmem = pl.BlockSpec(memory_space=pltpu.VMEM)
    size = 2 * sum(x.size for x in flat)
    return pl.pallas_call(
        functools.partial(join_kernel, [len(group) for group in groups]),
        in_specs=[vmem] * (len(flat) + len(marks)),
        out_specs=[vmem] * len(groups),
        out_shape=[
            jax.ShapeDtypeStruct((sum(x.shape[0] for x in group), group[0].shape[1]), BF)
            for group in groups
        ],
        compiler_params=pltpu.CompilerParams(vmem_limit_bytes=24 * 2**20),
        cost_estimate=pl.CostEstimate(flops=0, bytes_accessed=2 * size, transcendentals=0),
    )(*flat, *marks)


def gather(owns, marks):
    col_count = lax.axis_size("col")
    bits = row_bits(lax.axis_size("row"))
    half = col_count // 2
    rounds = len(bits) + 1
    state = [None] * len(owns)
    sent = owns[0]
    for tick in range(rounds + len(owns) - 1):
        groups, places = [], []
        for n in range(len(owns)):
            step = tick - n
            if step == 0:
                line = [sent] + [swap(sent, "col", d) for d in range(1, col_count)]
                state[n] = [line[:half], line[half:]]
            elif 0 < step < rounds:
                first, second = state[n]
                state[n] = [
                    [first, swap(first, "row", bits[step - 1])],
                    [second, swap(second, "row", bits[-step])],
                ]
            else:
                continue
            if step == rounds - 1:
                places.append((n, 0))
                groups.append(state[n][0] + state[n][1])
                continue
            for side in range(2):
                places.append((n, side))
                groups.append(state[n][side])
        if tick + 1 < len(owns):
            groups.append([owns[tick + 1]])
        joined = join(groups, tuple(marks[tick : tick + 1]))
        if tick + 1 < len(owns):
            sent = joined[-1]
        for (n, side), value in zip(places, joined):
            state[n][side] = value
        done = tick - rounds + 1
        if done >= 0:
            yield [state[done][0], swap(state[done][0], "row", 1)]


def invert_kernel(listed, lists, p0, p1, *refs):
    out_ref = refs[-1]
    pieces = (p0, p1)
    lines = out_ref.shape[1]
    count, _, wide = p0.shape
    line_ids = lax.broadcasted_iota(jnp.int32, (lines, wide), 0).astype(F32)
    lane_ids = lax.broadcasted_iota(jnp.int32, (LANES, wide), 0).astype(F32)
    for at, s in enumerate(lists):
        total = jnp.zeros((lines, 2 * LANES), F32)
        for n, piece in enumerate(pieces):
            left, right = [], []
            for m in range(count):
                code = piece[m, listed:, :].astype(F32)
                place = 1 + (n * count + m) * listed
                place = place + lax.broadcasted_iota(jnp.int32, (1, wide), 1)
                high = (place // LANES).astype(F32)
                low = (place % LANES).astype(F32)
                left.append(jnp.where(line_ids == code[2 * s : 2 * s + 1], 1.0, 0.0))
                on_lane = lane_ids == code[2 * s + 1 : 2 * s + 2]
                right.append(
                    jnp.concatenate(
                        [jnp.where(on_lane, high, 0.0), jnp.where(on_lane, low, 0.0)], 0
                    )
                )
            total += lax.dot_general(
                jnp.concatenate(left, 1).astype(BF),
                jnp.concatenate(right, 1).astype(BF),
                (((1,), (1,)), ((), ())),
                preferred_element_type=F32,
            )
        out_ref[at] = (total[:, :LANES] * LANES + total[:, LANES:]).astype(jnp.int32)


def invert(pieces, chunk, codes, lists, rows, marks):
    width = pieces[0].shape[1]
    pieces = [p.reshape(-1, chunk + codes, width) for p in pieces]
    vmem = pl.BlockSpec(memory_space=pltpu.VMEM)
    return pl.pallas_call(
        functools.partial(invert_kernel, chunk, lists),
        in_specs=[vmem] * 2 + [pl.BlockSpec(memory_space=pl.ANY)] * len(marks),
        out_specs=pl.BlockSpec(memory_space=pltpu.VMEM),
        out_shape=jax.ShapeDtypeStruct((len(lists), rows // LANES, LANES), jnp.int32),
        compiler_params=pltpu.CompilerParams(vmem_limit_bytes=16 * 2**20),
        cost_estimate=pl.CostEstimate(
            flops=10**9 * len(lists), bytes_accessed=4 * len(lists) * rows, transcendentals=0
        ),
    )(*pieces, *marks)


def tables_kernel(chunk, row_inv, col_inv, p0, p1, *refs):
    row_out, col_out, mark, source, target = refs[-5:]
    mark[...] = jnp.zeros_like(mark)
    step = 256
    width = col_out.shape[1]
    parts = width // LANES
    count = p0.shape[0]
    source[0 : 8 * parts, :] = jnp.zeros((8 * parts, LANES), F32)
    for n, piece in enumerate((p0, p1)):

        def fill(m, unused, n=n, piece=piece):
            values = piece[m, :chunk, :].astype(F32)
            base = parts * (1 + (n * count + m) * chunk)
            for q in range(parts):
                source[pl.ds(base + q, chunk, stride=parts), :] = values[
                    :, q * LANES : (q + 1) * LANES
                ]
            return unused

        lax.fori_loop(0, count, fill, 0)

    def pick(inv):
        batch = 16

        def line(h, unused):
            for first in range(0, LANES, batch):
                found = [
                    source[pl.ds(pl.multiple_of(parts * inv[h, first + u], parts), parts), :]
                    for u in range(batch)
                ]
                for u in range(batch):
                    target[
                        pl.ds(pl.multiple_of(parts * (h * LANES + first + u), parts), parts), :
                    ] = found[u]
            return unused

        lax.fori_loop(0, inv.shape[0], line, 0)

    pick(row_inv)
    for n in range(row_out.shape[1] // step):
        for q in range(parts):
            values = target[pl.ds(parts * n * step + q, step, stride=parts), :]
            row_out[q * LANES : (q + 1) * LANES, n * step : (n + 1) * step] = values.T.astype(BF)
    pick(col_inv)

    def drain(n, unused):
        at = pl.multiple_of(n * step, step)
        for q in range(parts):
            values = target[pl.ds(parts * at + q, step, stride=parts), :]
            col_out[pl.ds(at, step), q * LANES : (q + 1) * LANES] = values.astype(BF)
        return unused

    lax.fori_loop(0, col_out.shape[0] // step, drain, 0)


def tables(pieces, chunk, whole_chunk, row_inv, col_inv, marks):
    width = pieces[0].shape[1]
    pieces = [p.reshape(-1, whole_chunk, width) for p in pieces]
    count = pieces[0].shape[0]
    listed = 2 * count * chunk
    parts = width // LANES
    rows, cols = row_inv.size, col_inv.size
    vmem = pl.BlockSpec(memory_space=pltpu.VMEM)
    smem = pl.BlockSpec(memory_space=pltpu.SMEM)
    return pl.pallas_call(
        functools.partial(tables_kernel, chunk),
        in_specs=[smem, smem] + [vmem] * (2 + len(marks)),
        out_specs=[vmem] * 3,
        out_shape=[
            jax.ShapeDtypeStruct((width, rows), BF),
            jax.ShapeDtypeStruct((cols, width), BF),
            jax.ShapeDtypeStruct((8, LANES), F32),
        ],
        scratch_shapes=[
            pltpu.VMEM((parts * (listed + 8), LANES), F32),
            pltpu.VMEM((parts * (max(rows, cols) + 8), LANES), F32),
        ],
        compiler_params=pltpu.CompilerParams(vmem_limit_bytes=28 * 2**20),
        cost_estimate=pl.CostEstimate(
            flops=10**10, bytes_accessed=2 * width * (listed + rows + cols), transcendentals=0
        ),
    )(row_inv, col_inv, *pieces, *marks)


def block_kernel(ancestor, lower, diagonal, mark, held, arrived, left):
    mark[...] = jnp.zeros_like(mark)
    rows, cols = lower.shape
    step = 256
    wide = 512 if cols % 512 == 0 else cols
    row_start = lax.axis_index("row") * rows
    col_start = lax.axis_index("col") * cols
    ins, outs = [], []
    for n in range(0, rows, step):
        here = held.at[n : n + step]
        ins.append(pltpu.make_async_copy(ancestor.at[n : n + step], here, arrived.at[n // step]))
        outs.append(pltpu.make_async_copy(here, lower.at[n : n + step], left.at[n // step]))
    for copy in ins:
        copy.start()
    diagonal[...] = jnp.zeros_like(diagonal)
    for n in range(rows // step):
        ins[n].wait()
        row_first = row_start + n * step
        at = slice(n * step, (n + 1) * step)

        def strip(m, unused, row_first=row_first, at=at):
            first = pl.multiple_of(m * wide, wide)
            over = pl.ds(first, wide)
            col_first = col_start + first
            empty = row_first + step <= col_first

            @pl.when(empty)
            def none():
                held[at, over] = jnp.zeros((step, wide), BF)

            @pl.when(jnp.logical_not(empty) & (row_first < col_first + wide))
            def some():
                row_ids = row_first + lax.broadcasted_iota(jnp.int32, (step, wide), 0)
                col_ids = col_first + lax.broadcasted_iota(jnp.int32, (step, wide), 1)
                values = held[at, over].astype(F32)
                on = jnp.where(col_ids == row_ids, values, 0.0)
                diagonal[at, :] += jnp.sum(on, axis=1, keepdims=True)
                held[at, over] = jnp.where(col_ids < row_ids, values, 0.0).astype(BF)

            return unused

        lax.fori_loop(0, cols // wide, strip, 0)
        outs[n].start()
    for copy in outs:
        copy.wait()


def lower_block(ancestor):
    rows, cols = ancestor.shape
    anywhere = pl.BlockSpec(memory_space=pl.ANY)
    return pl.pallas_call(
        block_kernel,
        in_specs=[anywhere],
        out_specs=[pl.BlockSpec(memory_space=pltpu.HBM)] + [pl.BlockSpec(memory_space=pltpu.VMEM)] * 2,
        out_shape=[
            jax.ShapeDtypeStruct((rows, cols), BF),
            jax.ShapeDtypeStruct((rows, 1), F32),
            jax.ShapeDtypeStruct((8, LANES), F32),
        ],
        scratch_shapes=[
            pltpu.VMEM((rows, cols), BF),
            pltpu.SemaphoreType.DMA((rows // 256,)),
            pltpu.SemaphoreType.DMA((rows // 256,)),
        ],
        compiler_params=pltpu.CompilerParams(vmem_limit_bytes=24 * 2**20),
        cost_estimate=pl.CostEstimate(
            flops=rows * cols, bytes_accessed=4 * rows * cols, transcendentals=0
        ),
    )(ancestor)


def encode(values, lanes):
    high = values.astype(BF)
    low = (values - high.astype(F32)).astype(BF)
    both = jnp.concatenate([high, low], 1)
    return jnp.concatenate([both[:, n : n + lanes] for n in range(0, both.shape[1], lanes)], 0)


def decode(codes, width):
    rows = codes.shape[0] * codes.shape[1] // (2 * width)
    both = jnp.concatenate([codes[n : n + rows] for n in range(0, codes.shape[0], rows)], 1)
    both = both.astype(F32)
    return both[:, :width] + both[:, width:]


def terms_kernel(plan, block, diagonal, row_t, col, *refs):
    m_send, m_keep, direct, total, rounded, y = refs[-6:]
    i = pl.program_id(0)
    steps = pl.num_programs(0)
    rows = block.shape[0]
    owned = m_send.shape[2]
    tile = 2 * owned
    width = row_t.shape[0]
    coded = m_send.shape[1] - width
    core, swapped, offset, chip = [plan[steps + n] for n in range(4)]
    at_tile = pl.ds(pl.multiple_of(plan[i] * tile, tile), tile)
    values = col[at_tile, :]

    def mirrored(out, slot):
        term = jnp.dot(row_t[...], block[...], preferred_element_type=F32).astype(BF)
        out[slot + swapped, coded:, :] = term[:, :owned]
        out[slot + 1 - swapped, coded:, :] = term[:, owned:]

    @pl.when(i < steps // 2)
    def sent():
        mirrored(m_send, 2 * i)

    @pl.when(i >= steps // 2)
    def kept():
        mirrored(m_keep, 2 * i - steps)

    @pl.when(i == 0)
    def first():
        total[...] = jnp.dot(block[...], values, preferred_element_type=F32)

    @pl.when(i > 0)
    def later():
        total[...] += jnp.dot(block[...], values, preferred_element_type=F32)

    @pl.when(i == steps - 1)
    def last():
        cols = col.shape[0]
        for e in range(rows // owned):
            at = slice(e * owned, (e + 1) * owned)
            back = pl.multiple_of(jnp.clip(e * owned + offset, 0, cols - owned), owned)
            own = diagonal[at, :] * col[pl.ds(back, owned), :].astype(F32)
            term = total[at, :]
            rounded[at, :] = (term + 0.5 * own).astype(BF)
            direct[e] = (term + own).astype(BF)
        half = jnp.dot(row_t[...], rounded[...], preferred_element_type=F32)
        y[...] = half + half.T
        slots = m_send.shape[0]
        share = width // (2 * slots)
        for out, side in ((m_send, 1 - core), (m_keep, core)):
            for e in range(slots):
                start = pl.multiple_of((2 * (e ^ chip) + side) * share, share)
                out[e, :coded, :] = encode(y[pl.ds(start, share), :], owned)


def terms(plan, lower, diagonal, row_t, col, owned, marks):
    rows, cols = lower.shape
    width = col.shape[1]
    steps = cols // (2 * owned)
    count = rows // owned
    everything = [
        pl.BlockSpec(x.shape, lambda i, plan, x=x: (0,) * x.ndim) for x in (diagonal, row_t, col)
    ]
    anywhere = pl.BlockSpec(memory_space=pl.ANY)
    d_spec = pl.BlockSpec((count, owned, width), lambda i, plan: (0, 0, 0))
    coded = 2 * width * width // cols
    m_spec = pl.BlockSpec((steps, coded + width, owned), lambda i, plan: (0, 0, 0))
    grid_spec = pltpu.PrefetchScalarGridSpec(
        num_scalar_prefetch=1,
        grid=(steps,),
        in_specs=[pl.BlockSpec((rows, 2 * owned), lambda i, plan: (0, plan[i]))]
        + everything
        + [anywhere] * len(marks),
        out_specs=[m_spec, m_spec, d_spec],
        scratch_shapes=[
            pltpu.VMEM((rows, width), F32),
            pltpu.VMEM((rows, width), BF),
            pltpu.VMEM((width, width), F32),
        ],
    )
    return pl.pallas_call(
        terms_kernel,
        grid_spec=grid_spec,
        out_shape=[
            jax.ShapeDtypeStruct((steps, coded + width, owned), BF),
            jax.ShapeDtypeStruct((steps, coded + width, owned), BF),
            jax.ShapeDtypeStruct((count, owned, width), BF),
        ],
        compiler_params=pltpu.CompilerParams(vmem_limit_bytes=34 * 2**20),
        cost_estimate=pl.CostEstimate(
            flops=5 * rows * cols * width, bytes_accessed=2 * rows * cols, transcendentals=0
        ),
    )(plan, lower, diagonal, row_t, col, *marks)


def tree_sum(values):
    values = [x.astype(F32) for x in values]
    while len(values) > 1:
        values = [a + b for a, b in zip(values[::2], values[1::2])]
    return values[0]


def sums_kernel(width, counts, outs, marks, *refs):
    ins, outs_refs = refs[: len(refs) - len(outs) - marks], refs[len(refs) - len(outs) :]
    groups, at = [], 0
    for count in counts:
        groups.append(ins[at : at + count])
        at += count
    for ref, pieces in zip(outs_refs, outs):
        for place, group, slot, low, high, coded in pieces:
            addends = [x[slot, low:high] for x in groups[group]]
            if ref.dtype == F32 and coded:
                ref[place] = tree_sum([decode(x, ref.shape[2]) for x in addends])
                continue
            if coded:
                total = tree_sum([decode(x[:coded], width) for x in addends])
                ref[place, :coded] = encode(total, ref.shape[2])
            ref[place, coded:] = tree_sum([x[coded:] for x in addends]).astype(ref.dtype)


def sums(groups, outs, width, marks=()):
    flat = [x for group in groups for x in group]
    shapes = []
    for pieces in outs:
        _, group, _, low, high, coded = pieces[0]
        like = groups[group][0]
        rows, lanes, dtype = high - low, like.shape[2], like.dtype
        if coded == rows:
            rows, lanes, dtype = rows * lanes // (2 * width), width, F32
        shapes.append(jax.ShapeDtypeStruct((len(pieces), rows, lanes), dtype))
    vmem = pl.BlockSpec(memory_space=pltpu.VMEM)
    size = sum(x.size for x in flat)
    return pl.pallas_call(
        functools.partial(sums_kernel, width, [len(group) for group in groups], outs, len(marks)),
        in_specs=[vmem] * len(flat) + [pl.BlockSpec(memory_space=pl.ANY)] * len(marks),
        out_specs=[vmem] * len(outs),
        out_shape=shapes,
        compiler_params=pltpu.CompilerParams(vmem_limit_bytes=16 * 2**20),
        cost_estimate=pl.CostEstimate(flops=size, bytes_accessed=3 * size, transcendentals=0),
    )(*flat, *marks)


def mirrored_share(m_send, m_keep, paths, width):
    col_bits = lax.axis_size("col").bit_length() - 1
    rows, owned = m_keep.shape[1:]
    coded = rows - width
    part = width // paths
    cuts = [0] + [coded + part * (path + 1) for path in range(paths)]
    bits = row_bits(lax.axis_size("row"))
    slots = [list(range(len(m_keep))) for _ in range(paths)]
    groups = [(m_keep, swap(m_send, "row", 1))]
    for n in range(col_bits):
        outs = []
        chosen_bits = []
        for path in range(paths):
            place = col_bits - 1 - n if path else n
            chosen_bits.append(bits[place])
            low, high = cuts[path : path + 2]
            group = 0 if n == 0 else path
            if n:
                low, high = 0, high - low
            codes = 0 if path else coded
            for send in (True, False):
                chosen = [i for i, e in enumerate(slots[path]) if bool(e >> place & 1) == send]
                outs.append([(p, group, i, low, high, codes) for p, i in enumerate(chosen)])
            slots[path] = [e for e in slots[path] if not e >> place & 1]
        made = yield groups, outs
        groups = [
            (made[2 * path + 1], swap(made[2 * path], "row", chosen_bits[path]))
            for path in range(paths)
        ]
    own = []
    for path in range(paths):
        first = 0 if path else coded
        own.append((path, path, 0, first, first + part, 0))
    own, y = yield groups, [own, [(0, 0, 0, 0, coded, coded)]]
    return to_owner(own.reshape(width, owned)), y


def diagonal_sum(ys, early):
    y = jnp.concatenate(ys, 0)[:, None]
    bits = []
    bit = lax.axis_size("row") // 2
    while bit:
        bits.append(bit)
        bit //= 2
    for n, bit in enumerate(bits):
        if n == (0 if early else len(bits) - 1):
            along = 1
            while along < lax.axis_size("col"):
                y = y + swap(y, "col", along)
                along *= 2
        other = swap(y, "row", bit)
        low = (lax.axis_index("row") & bit) == 0
        both = [jnp.where(low, y, other), jnp.where(low, other, y)]
        y = jnp.stack(both, 2).reshape(y.shape[0], -1, *y.shape[2:])
    return y.reshape(y.shape[0], -1, y.shape[3])


class Rounds:
    def __init__(self, width, *chains):
        self.width = width
        self.chains = chains
        self.results = [None] * len(chains)
        self.jobs = {}
        for n, chain in enumerate(chains):
            self.send(n, None)

    def send(self, n, values):
        try:
            self.jobs[n] = self.chains[n].send(values)
        except StopIteration as end:
            self.jobs.pop(n, None)
            self.results[n] = end.value

    def advance(self, *marks):
        groups, outs = [], []
        for job_groups, job_outs in self.jobs.values():
            for pieces in job_outs:
                outs.append([(p, group + len(groups), *rest) for p, group, *rest in pieces])
            groups += job_groups
        made = sums(groups, outs, self.width, marks)
        at = 0
        for n, (_, job_outs) in list(self.jobs.items()):
            self.send(n, made[at : at + len(job_outs)])
            at += len(job_outs)
        return made[-1]

    def finish(self):
        while self.jobs:
            self.advance()
        return self.results


def reversed_bits(value, bits):
    return sum(((value >> n) & 1) << (bits - 1 - n) for n in range(bits))


def to_owner(x):
    row_count = lax.axis_size("row")
    col_count = lax.axis_size("col")
    bits = col_count.bit_length() - 1
    pairs = []
    for row in range(row_count):
        for col in range(col_count):
            place = (row // 2) ^ reversed_bits(col, bits)
            pairs.append((row * col_count + col, (2 * col + row % 2) * col_count + place))
    return lax.ppermute(x, ("row", "col"), pairs)


def finish_kernel(member, *refs):
    out = refs[-1]
    owned = out.shape[0]
    sibs = member.shape[0]
    width = out.shape[1] // sibs
    s = 0
    for n in range(0, len(refs) - 1, 2):
        parts, mirrored = refs[n : n + 2]
        for at in range(0, mirrored.shape[0], width):
            over = slice(at, at + width)
            product = mirrored[over, :].astype(F32).T
            for m in range(parts.shape[0]):
                product = product + parts[m, :, over].astype(F32)
            listed = jnp.broadcast_to(member[s : s + 1, :].astype(F32), (LANES, owned)).T
            for q in range(0, width, LANES):
                out[:, s * width + q : s * width + q + LANES] = jnp.where(
                    listed > 0.5, -product[:, q : q + LANES], 0.0
                ).astype(BF)
            s += 1


def finish(member, shares, width):
    sibs, owned = member.shape
    vmem = pl.BlockSpec(memory_space=pltpu.VMEM)
    flat = [x for share in shares for x in share]
    return pl.pallas_call(
        finish_kernel,
        in_specs=[vmem] * (1 + len(flat)),
        out_specs=vmem,
        out_shape=jax.ShapeDtypeStruct((owned, sibs * width), BF),
        compiler_params=pltpu.CompilerParams(vmem_limit_bytes=24 * 2**20),
        cost_estimate=pl.CostEstimate(
            flops=4 * owned * sibs * width,
            bytes_accessed=8 * owned * sibs * width,
            transcendentals=0,
        ),
    )(member, *flat)


def per_device(ancestor, panels, row_index, diag_inverse):
    row_count = lax.axis_size("row")
    col_count = lax.axis_size("col")
    assert row_count == 2 * col_count
    block_rows, block_cols = ancestor.shape
    sib_count, listed, width = panels.shape
    owned = block_rows // col_count
    row_place = lax.axis_index("row")
    col_place = lax.axis_index("col")
    core = row_place % 2
    chip = row_place // 2
    col_bits = col_count.bit_length() - 1
    row_lines, col_lines, own_lines = block_rows // LANES, block_cols // LANES, owned // LANES
    mixed = chip ^ sum(((col_place >> n) & 1) << (col_bits - 1 - n) for n in range(col_bits))
    pairs = [(2 * n ^ mixed) // 2 for n in range(col_count // 2)]
    plan = jnp.stack(
        [n + (1 - core) * (col_count // 2) for n in pairs]
        + [n + core * (col_count // 2) for n in pairs]
        + [core, mixed % 2, row_place * block_rows - col_place * block_cols, chip]
    ).astype(jnp.int32)

    codes = jnp.stack([row_index // LANES, row_index % LANES], 1).astype(BF)
    codes = codes.reshape(-1, listed)
    code_rows = -(-len(codes) // 16) * 16
    codes = jnp.pad(
        codes, ((0, code_rows - len(codes)), (0, width - listed)), constant_values=-1
    )
    owns = [jnp.concatenate([panels[0], codes], 0)] + [panels[s] for s in range(1, sib_count)]
    chunks = [listed + code_rows] + [listed] * (sib_count - 1)

    lower, diagonal, mark = lower_block(ancestor)
    marks = [mark] * (len(row_bits(row_count)) + 1)
    gathered = gather(owns, marks)
    both, direct = [], []
    row_inv = col_inv = None
    members = []
    for s in range(sib_count):
        pieces = next(gathered)
        if s == 0:
            coded = pieces
            inverse = invert(coded, listed, code_rows, [0], block_rows * row_count, [])
        elif s == 1:
            rest = list(range(1, sib_count))
            inverse = invert(coded, listed, code_rows, rest, block_rows * row_count, [mark])
        if s < 2:
            row_inv = lax.dynamic_slice_in_dim(inverse, row_place * row_lines, row_lines, 1)
            col_inv = lax.dynamic_slice_in_dim(inverse, col_place * col_lines, col_lines, 1)
            own_inv = lax.dynamic_slice_in_dim(
                inverse, row_place * row_lines + col_place * own_lines, own_lines, 1
            )
            members.append(own_inv.reshape(-1, owned))
        at = max(s - 1, 0)
        before = [chain.advance() for chain in both if chain.jobs] + direct[:-1]
        row_t, col, mark = tables(pieces, listed, chunks[s], row_inv[at], col_inv[at], before)
        marks.append(mark)
        before = [chain.advance(mark) for chain in both[-1:] if chain.jobs]
        before += [chain.results[0][0] for chain in both if not chain.jobs]
        m_send, m_keep, parts = terms(plan, lower, diagonal, row_t, col, owned, before)
        paths = 2
        both.append(Rounds(width, mirrored_share(m_send, m_keep, paths, width)))
        direct.append(lax.all_to_all(parts, "col", 0, 0, tiled=True))
    both[-1].advance(*direct[-2:-1])
    mark = both[-1].advance()
    for chain in both[:-1]:
        while chain.jobs:
            chain.advance(mark)
    while both[-1].jobs:
        both[-1].advance(*direct[-1:])
    shares, ys = [], []
    for s in range(sib_count):
        mirrored, y = both[s].results[0]
        shares.append((direct[s], mirrored))
        ys.append(y)
    diags = jnp.concatenate([diagonal_sum(ys[:-1], True), diagonal_sum(ys[-1:], False)], 0)
    return finish(jnp.concatenate(members, 0), shares, width), diag_inverse + diags


def solution(mesh):
    in_specs = (P("row", "col"), P(None, ("row", "col"), None), P(None, ("row", "col")), P())
    out_specs = (P(("row", "col"), None), P())
    return jax.shard_map(
        per_device, mesh=mesh, in_specs=in_specs, out_specs=out_specs, check_vma=False
    )
```
